32 devices in a mesh: row: 4 (over z), col: 8 (over y, x, core).
Axes of the slice: x: 2, y: 2, z: 4, core: 2. Of those that a mesh axis runs over, the one named last changes fastest.
Arguments:
- right_side: float32 [3, 4096, 4096], P(None, 'row', 'col'), may hold values from -6 to 6
- panel_t: float32 [2, 1024, 3, 4096], P(None, 'col', None, 'row'), may hold values from -0.1875 to 0.1875
- inverse_blocks: float32 [2, 1024, 1024], P(None, 'row'), as said below
Outputs:
- solved: float32 [2, 1024, 4096], P(None, 'row', 'col')
- remaining: float32 [3, 4096, 4096], P(None, 'row', 'col')
The draws below stay inside these ranges and needn't reach their ends.
Inputs may be any that keep to these rules, and one draw needn't show every extreme that they name: Each inverse_blocks[k] is lower triangular with a diagonal between 0.5 and 2.
All inputs are finite; a program needn't handle non-finite values.
Results may differ from the reference program's by a relative error of at most 0.0001.
Values sent between devices are 32-bit elements; how exact they have to be, the bound alone decides.
No kernel may reach another device: no remote copies, remote signals or barrier semaphores. Data moves between devices by JAX's collectives and lax.ppermute only.
A program may use at most 128 MiB of HBM per device.

```python
import jax
import jax.numpy as jnp
from jax import lax

NB = 1024
R = 4096
BLK_DEV = 3
N_ROW = 4


def draw_inverse_blocks(key, part):
    key = jax.random.fold_in(key, 7)
    first, second = jax.random.split(key)
    shape = (2, NB, NB)
    rows = lax.broadcasted_iota(jnp.int32, shape, 1)
    cols = lax.broadcasted_iota(jnp.int32, shape, 2)
    diag = jax.random.uniform(first, shape, jnp.float32, 0.5, 2.0)
    off = jax.random.normal(second, shape, jnp.float32) / jnp.sqrt(jnp.float32(NB))
    return jnp.where(rows == cols, diag, jnp.where(rows > cols, off, jnp.float32(0.0)))


def level_of(key, shape, shards, smallest, top_value):
    factor_of, own = 1.0, jax.random.fold_in(key, 6)
    for position, shards_of in shards:
        heights = jnp.exp(jax.random.uniform(jax.random.fold_in(own, position), (shards_of,), jnp.float32, smallest / len(shards), top_value / len(shards)))
        factor_of = factor_of * jnp.repeat(heights, shape[position] // shards_of).reshape([-1 if axis == position else 1 for axis in range(len(shape))])
    return factor_of


def normal_values(own_key, extent, deviation, reach, shards=(), held_as=jnp.bfloat16):
    gain = level_of(own_key, extent, shards, -0.22, 0.18) if shards else 1.0
    drawn = jax.random.normal(own_key, extent, jnp.float32) * deviation * gain
    return jnp.minimum(jnp.maximum(drawn, -reach), reach).astype(held_as)


def setup_inputs(seed: int = 0) -> dict:
    key_list = jax.random.split(jax.random.key(seed), 4)
    return {
        "right_side": normal_values(key_list[0], (BLK_DEV, N_ROW * NB, R), 1.0, 6.0, ((1, 4), (2, 8)), jnp.float32),
        "panel_t": normal_values(key_list[1], (2, NB, BLK_DEV, N_ROW * NB), NB ** -0.5, 0.1875, ((1, 8), (3, 4)), jnp.float32),
        "inverse_blocks": draw_inverse_blocks(jax.random.fold_in(key_list[3], 71), 0),
    }


def reference(right_side, panel_t, inverse_blocks):
    total = right_side.shape[0] * right_side.shape[1]
    matrix = right_side.reshape(total, R)
    block_of = jnp.arange(total, dtype=jnp.int32) // NB
    results = []
    for k in range(2):
        top = matrix[k * NB:(k + 1) * NB]
        solved_k = jnp.dot(inverse_blocks[k], top, precision=lax.Precision.HIGHEST, preferred_element_type=jnp.float32)
        results.append(solved_k)
        column = panel_t[k].reshape(NB, total).T
        update = jnp.dot(column, solved_k, precision=lax.Precision.HIGHEST, preferred_element_type=jnp.float32)
        matrix = matrix - jnp.where((block_of > k)[:, None], update, jnp.float32(0.0))
    return jnp.stack(results), matrix.reshape(right_side.shape)
```

```python
import functools

import jax
import jax.numpy as jnp
from jax import lax
from jax.experimental import pallas as pl
from jax.experimental.pallas import tpu as pltpu
from jax.sharding import PartitionSpec as P

LAG = 1


def from_root(value, axis, source):
    kept = jnp.where(lax.axis_index(axis) == source, value, 0).astype(value.dtype)
    return lax.psum(kept, axis)


def plain_body(right_side, panel_t, inverse_blocks):
    grid_rows = lax.axis_size("row")
    my_row = lax.axis_index("row")
    blocks_here = right_side.shape[0]
    global_block = jnp.arange(blocks_here, dtype=jnp.int32) * grid_rows + my_row
    results = []
    for k in range(2):
        owner = k % grid_rows
        top = from_root(right_side[k // grid_rows], "row", owner)
        share = jnp.dot(
            inverse_blocks[k],
            top,
            precision=lax.Precision.HIGHEST,
            preferred_element_type=jnp.float32,
        )
        results.append(share)
        solved_k = lax.all_gather(share, "row", axis=0, tiled=True)
        update = jnp.einsum(
            "cji,cr->jir",
            lax.all_gather(panel_t[k], "col", axis=0, tiled=True),
            solved_k,
            precision=lax.Precision.HIGHEST,
            preferred_element_type=jnp.float32,
        )
        keep_mask = (global_block > k)[:, None, None]
        right_side = right_side - jnp.where(keep_mask, update, jnp.float32(0.0))
    return (jnp.stack(results), right_side)


def split(x):
    hi = x.astype(jnp.bfloat16)
    return hi, (x - hi.astype(jnp.float32)).astype(jnp.bfloat16)


def dot3(a, b_hi, b_lo):
    a_hi, a_lo = split(a)
    dot = functools.partial(jnp.dot, preferred_element_type=jnp.float32)
    return dot(a_hi, b_hi) + (dot(a_hi, b_lo) + dot(a_lo, b_hi))


def update(rhs, panels, sources, k, first_piece=0, alias=False, all_rows=False):
    blocks, rows, cols = rhs.shape
    width = panels[0].shape[3]
    tile = min(256, rows)
    steps = rows // tile
    depth = sum(c.shape[0] for c in sources[0])
    pieces = depth // width
    arrays = []
    for chunks in sources:
        for chunk in chunks:
            if not any(chunk is a for a in arrays):
                arrays.append(chunk)
    where = [[next(i for i, a in enumerate(arrays) if a is c) for c in chunks] for chunks in sources]
    heights = [c.shape[0] for c in sources[0]]
    starts = [sum(p.shape[1] for p in panels[:i]) for i in range(len(panels))]

    def kernel(rhs_ref, *refs):
        panel_refs, refs = refs[: len(panels)], refs[len(panels):]
        chunk_refs, refs = refs[: len(arrays)], refs[len(arrays):]
        out_ref, whole, x_hi, x_lo, sems = refs
        step = pl.program_id(0)
        my_row = lax.axis_index("row")

        @pl.when(step == 0)
        def _():
            for row, ids in enumerate(where):

                @pl.when((my_row == row) if not all_rows else (row == 0))
                def _():
                    copies = []
                    at = 0
                    for n, i in enumerate(ids):
                        copies.append(
                            pltpu.make_async_copy(
                                chunk_refs[i], whole.at[pl.ds(at, heights[n])], sems.at[n]
                            )
                        )
                        at += heights[n]
                    for copy in copies:
                        copy.start()
                    for copy in copies:
                        copy.wait()

            hi, lo = split(whole[...])
            x_hi[...] = hi
            x_lo[...] = lo

        j = step // steps
        if all_rows:
            active = j >= 0
        else:
            active = j * len(sources) + my_row > k

        for i, panel in enumerate(panel_refs):
            inside = (j >= starts[i]) & (j < starts[i] + panels[i].shape[1])

            @pl.when(active & inside)
            def _():
                left = jnp.concatenate([panel[p, 0] for p in range(pieces)], axis=1)
                out_ref[0] = rhs_ref[0] - dot3(left, x_hi[...], x_lo[...])

        @pl.when(jnp.logical_not(active))
        def _():
            out_ref[0] = rhs_ref[0]

    def panel_spec(i):
        last = panels[i].shape[1] * steps - 1

        def index(s):
            at = jnp.clip(s - starts[i] * steps, 0, last)
            return (first_piece // pieces, at // steps, at % steps, 0)

        return pl.BlockSpec((pieces, 1, tile, width), index)

    block = pl.BlockSpec((1, tile, cols), lambda s: (s // steps, s % steps, 0))
    flops = 2 * 3 * blocks * rows * depth * cols
    moved = 4 * (2 * blocks * rows * cols + blocks * rows * depth + depth * cols)
    return pl.pallas_call(
        kernel,
        grid=(blocks * steps,),
        in_specs=[block]
        + [panel_spec(i) for i in range(len(panels))]
        + [pl.BlockSpec(memory_space=pl.ANY)] * len(arrays),
        out_specs=block,
        out_shape=jax.ShapeDtypeStruct(rhs.shape, rhs.dtype),
        scratch_shapes=[
            pltpu.VMEM((depth, cols), jnp.float32),
            pltpu.VMEM((depth, cols), jnp.bfloat16),
            pltpu.VMEM((depth, cols), jnp.bfloat16),
            pltpu.SemaphoreType.DMA((len(heights),)),
        ],
        input_output_aliases={0: 0} if alias else {},
        compiler_params=pltpu.CompilerParams(vmem_limit_bytes=32 * 2**20),
        cost_estimate=pl.CostEstimate(flops=flops, bytes_accessed=moved, transcendentals=0),
    )(rhs, *panels, *arrays)


def body(right_side, panel_t, inverse_blocks):
    n_row = lax.axis_size("row")
    my_row = lax.axis_index("row")
    share = inverse_blocks.shape[1]
    depth = inverse_blocks.shape[2]
    n = depth // share

    def send(value, pairs):
        return lax.ppermute(value, "row", pairs)

    def high(a, b):
        return jnp.dot(a, b, precision=lax.Precision.HIGH, preferred_element_type=jnp.float32)

    panel = jnp.transpose(panel_t, (0, 2, 3, 1))
    head0 = lax.all_gather(panel[0, :1], "col")
    tail0 = lax.all_gather(panel[0, 1:], "col")
    whole1 = lax.all_gather(panel[1], "col")

    inverse0 = [inverse_blocks[0]]
    for q in range(1, n):
        inverse0.append(send(inverse_blocks[0][:, : (q + 1) * share], [(q, 0)]))
    inverse1 = []
    for q in range(n):
        own = inverse_blocks[1][:, : (q + 1) * share]
        inverse1.append(own if q == 1 else send(own, [(q, 1)]))

    top = right_side[0]
    line = [(r, r + 1) for r in range(n_row - 1)]
    slots = 2 * n + LAG * (n_row - 2)
    received = []
    first = []
    second = []
    lowered = None
    for t in range(slots):
        value = received[t - LAG] if t >= LAG else None
        q = t - LAG - n
        if 0 <= q < n:
            if q == 0:
                lowered = update(
                    right_side[:1], [head0], [received[:n]], 0, all_rows=True
                )[0]
            second.append(high(inverse1[q], lowered[: (q + 1) * share]))
            value = jnp.where(my_row == 1, second[q], value)
        if t < n:
            first.append(high(inverse0[t][:, : (t + 1) * share], top[: (t + 1) * share]))
            value = first[t] if value is None else jnp.where(my_row == 0, first[t], value)
        received.append(send(value, line))
    back = []
    for q in range(0, n, 2):
        pair = send(jnp.concatenate(second[q:q + 2], axis=0), [(1, 0)])
        back += [pair[:share], pair[share:]]

    chunks0 = [first] + [received[LAG * (r - 1):][:n] for r in range(1, n_row)]
    chunks1 = [back, second] + [received[n + LAG * (r - 1):][:n] for r in range(2, n_row)]

    remaining = update(right_side, [head0, tail0], chunks0, 0)
    early = n - 1
    remaining = update(remaining, [whole1], [c[:early] for c in chunks1], 1, alias=True)
    per = share // panel.shape[3]
    remaining = update(
        remaining, [whole1], [c[early:] for c in chunks1], 1, first_piece=early * per, alias=True
    )

    solved = []
    for chunks in (chunks0, chunks1):
        mine = chunks[0][0]
        for r in range(1, n_row):
            mine = jnp.where(my_row == r, chunks[r][r], mine)
        solved.append(mine)
    return (jnp.stack(solved), remaining)


def choose(right_side, panel_t, inverse_blocks):
    if panel_t.shape[1] % 128 == 0 and inverse_blocks.shape[1] % 256 == 0:
        return body(right_side, panel_t, inverse_blocks)
    return plain_body(right_side, panel_t, inverse_blocks)


def solution(mesh):
    return jax.shard_map(
        choose,
        mesh=mesh,
        in_specs=(P(None, "row", "col"), P(None, "col", None, "row"), P(None, "row", None)),
        out_specs=(P(None, "row", "col"), P(None, "row", "col")),
        check_vma=False,
    )
```

```python
import functools
import math

import jax
import jax.numpy as jnp
from jax import lax
from jax.experimental import pallas as pl
from jax.experimental.pallas import tpu as pltpu
from jax.sharding import PartitionSpec as P

def from_root(value, axis, source):
    kept = jnp.where(lax.axis_index(axis) == source, value, 0).astype(value.dtype)
    return lax.psum(kept, axis)


def plain_body(right_side, panel_t, inverse_blocks):
    grid_rows = lax.axis_size("row")
    my_row = lax.axis_index("row")
    blocks_here = right_side.shape[0]
    global_block = jnp.arange(blocks_here, dtype=jnp.int32) * grid_rows + my_row
    results = []
    for k in range(2):
        owner = k % grid_rows
        top = from_root(right_side[k // grid_rows], "row", owner)
        share = jnp.dot(
            inverse_blocks[k],
            top,
            precision=lax.Precision.HIGHEST,
            preferred_element_type=jnp.float32,
        )
        results.append(share)
        solved_k = lax.all_gather(share, "row", axis=0, tiled=True)
        update = jnp.einsum(
            "cji,cr->jir",
            lax.all_gather(panel_t[k], "col", axis=0, tiled=True),
            solved_k,
            precision=lax.Precision.HIGHEST,
            preferred_element_type=jnp.float32,
        )
        keep_mask = (global_block > k)[:, None, None]
        right_side = right_side - jnp.where(keep_mask, update, jnp.float32(0.0))
    return (jnp.stack(results), right_side)


VMEM_LIMIT = 20 * 2**20
LAG = 2


def split(x):
    hi = x.astype(jnp.bfloat16)
    return hi, (x - hi.astype(jnp.float32)).astype(jnp.bfloat16)


def dot3(a, b_hi, b_lo):
    a_hi, a_lo = split(a)
    dot = functools.partial(jnp.dot, preferred_element_type=jnp.float32)
    return dot(a_hi, b_hi) + (dot(a_hi, b_lo) + dot(a_lo, b_hi))


def in_vmem(x):
    return pltpu.with_memory_space_constraint(x, pltpu.VMEM)


ANY = pl.BlockSpec(memory_space=pl.ANY)
WHOLE = pl.BlockSpec(memory_space=pltpu.VMEM)


def distinct(sources):
    arrays = []
    where = []
    for chunks in sources:
        ids = []
        for chunk in chunks:
            for i, a in enumerate(arrays):
                if a is chunk:
                    break
            else:
                i = len(arrays)
                arrays.append(chunk)
            ids.append(i)
        where.append(ids)
    return arrays, where


def params():
    return pltpu.CompilerParams(vmem_limit_bytes=VMEM_LIMIT)


def cost():
    return pl.CostEstimate(flops=1024, bytes_accessed=1024, transcendentals=0)


def in_hbm(x):
    return pltpu.with_memory_space_constraint(x, pltpu.HBM)


def PIN(x):
    return x


def turn(panel, slabs, after):
    _, blocks, depth, rows = panel.shape
    k0, j0 = slabs[0]
    start = k0 * blocks + j0

    def kernel(in_ref, *refs):
        refs[-1][0] = in_ref[0, 0].T

    def index(s):
        at = start + s
        return (at // blocks, at % blocks, 0, 0)

    return pl.pallas_call(
        kernel,
        grid=(len(slabs),),
        in_specs=[pl.BlockSpec((1, 1, depth, rows), index)] + [ANY] * len(after),
        out_specs=pl.BlockSpec((1, rows, depth), lambda s: (s, 0, 0)),
        out_shape=jax.ShapeDtypeStruct((len(slabs), rows, depth), panel.dtype),
        compiler_params=params(),
        cost_estimate=cost(),
    )(in_hbm(panel), *after)


def full(shape):
    return pl.BlockSpec(shape, lambda *_: (0,) * len(shape))


def copies(sources, shapes, plan, after):
    count = len(sources)

    def kernel(*refs):
        outs, sems = refs[-1 - len(shapes):-1], refs[-1]
        moves = plan(refs[:count], outs)
        for act in (True, False):
            for n, (condition, source, target) in enumerate(moves):

                def go():
                    copy = pltpu.make_async_copy(source, target, sems.at[n])
                    copy.start() if act else copy.wait()

                if condition is None:
                    go()
                else:
                    pl.when(condition)(go)

    return pl.pallas_call(
        kernel,
        grid=(1,),
        in_specs=[ANY] * (count + len(after)),
        out_specs=[full(shape) for shape in shapes],
        out_shape=[jax.ShapeDtypeStruct(shape, jnp.float32) for shape in shapes],
        scratch_shapes=[pltpu.SemaphoreType.DMA((16,))],
        compiler_params=params(),
        cost_estimate=cost(),
    )(*[in_hbm(x) for x in sources], *after)


def slot(inverse, k, rhs, received, top, part, after):
    if len(inverse) == 1:
        _, chunk, _ = inverse[0].shape
        depth = (part - LAG - k * (inverse[0].shape[2] // chunk) + 1) * chunk
        specs = [pl.BlockSpec((1, chunk, depth), lambda s: (k, 0, 0))]
        inverse = [in_hbm(inverse[0])]
    else:
        half, depth = inverse[0].shape
        chunk = 2 * half
        specs = [full((half, depth))] * 2
    cols = received.shape[1]
    tops = [] if top is None else [in_hbm(top)]

    def kernel(*refs):
        inverse_refs, refs = refs[: len(inverse)], refs[len(inverse):]
        received_ref, refs = refs[0], refs[1:]
        rhs_refs, refs = refs[: len(rhs)], refs[len(rhs):]
        out_ref, whole, sems = refs[-3:]
        my_row = lax.axis_index("row")

        def move(source, target, n=0):
            return pltpu.make_async_copy(source, target, sems.at[n])

        if tops:

            @pl.when(my_row == 0)
            def _():
                copy = move(refs[0].at[0, pl.ds(part * chunk, chunk)], out_ref)
                copy.start()
                copy.wait()

        @pl.when(my_row == 1)
        def _():
            moves = []
            for n, ref in enumerate(rhs_refs):
                if len(rhs) == 1 and rhs[0].ndim == 3:
                    moves.append(move(ref.at[0, pl.ds(0, depth)], whole))
                else:
                    moves.append(move(ref, whole.at[pl.ds(n * chunk, chunk)], n))
            for copy in moves:
                copy.start()
            for copy in moves:
                copy.wait()
            high, low = split(whole[...])
            if len(inverse) == 1:
                out_ref[...] = dot3(inverse_refs[0][0], high, low)
            else:
                core = lax.rem(lax.axis_index("col"), 2)
                for p, ref in enumerate(inverse_refs):
                    at = pl.multiple_of((core if p == 0 else 1 - core) * half, half)
                    out_ref[pl.ds(at, half)] = dot3(ref[...], high, low)

        @pl.when(my_row > 1)
        def _():
            copy = move(received_ref, out_ref)
            copy.start()
            copy.wait()

    return pl.pallas_call(
        kernel,
        grid=(1,),
        in_specs=specs + [ANY] * (1 + len(rhs) + len(tops) + len(after)),
        out_specs=full((chunk, cols)),
        out_shape=jax.ShapeDtypeStruct((chunk, cols), jnp.float32),
        scratch_shapes=[
            pltpu.VMEM((depth, cols), jnp.float32),
            pltpu.SemaphoreType.DMA((len(rhs),)),
        ],
        compiler_params=params(),
        cost_estimate=cost(),
    )(*inverse, received, *rhs, *tops, *after)


def fetch(where, refs, whole, sems, height, my_row):
    for row, ids in enumerate(where):

        @pl.when((my_row == row) | (len(where) == 1))
        def _():
            copies = [
                pltpu.make_async_copy(refs[i], whole.at[pl.ds(n * height, height)], sems.at[n])
                for n, i in enumerate(ids)
            ]
            for copy in copies:
                copy.start()
            for copy in copies:
                copy.wait()


def update(rhs, k, parts, sources, after, js, first=False, fresh=False, solved=None):
    heads = rhs if isinstance(rhs, list) else [rhs]
    _, rows, cols = heads[0].shape
    blocks = sum(h.shape[0] for h in heads)
    tile = 512
    steps = rows // tile
    arrays, where = distinct(sources)
    height = arrays[0].shape[0]
    depth = height * len(where[0])
    given, given_where = distinct([a + b for a, b in zip(*solved)]) if solved else ([], [])
    last = len(given) > 0
    panels = []
    panel_specs = []
    spans = []
    for panel, begin, end, piece, piece_end, _, slab in parts:

        def place(s, begin=begin, end=end, slab=slab):
            at = jnp.clip(s - (begin - js[0]) * steps, 0, (end - begin) * steps - 1)
            return slab + at // steps, at % steps

        at = len(panels)
        if isinstance(panel, tuple):
            for group in range(piece // 2, piece_end // 2):

                def index(s, col, group=group, place=place):
                    return (lax.bitwise_xor(col[0] // 2, group), *place(s), 0)

                for one in panel:
                    panels.append(one)
                    panel_specs.append(pl.BlockSpec((1, 1, tile, one.shape[3]), index))
        else:
            count = piece_end - piece

            def index(s, col, which=piece // count, place=place):
                return (which, *place(s), 0)

            panels.append(panel)
            panel_specs.append(pl.BlockSpec((count, 1, tile, panel.shape[3]), index))
        spans.append((at, len(panels)))

    def kernel(col_ref, *refs):
        rhs_refs, refs = refs[: len(heads)], refs[len(heads):]
        panel_refs, refs = refs[: len(panels)], refs[len(panels):]
        chunk_refs, refs = refs[: len(arrays)], refs[len(arrays):]
        given_refs, refs = refs[: len(given)], refs[len(given):]
        refs = refs[len(after):]
        out_ref, refs = refs[0], refs[1:]
        if last:
            solved_ref, refs = refs[0], refs[1:]
        whole, x_hi, x_lo, sems = refs[:4]
        step = pl.program_id(0)
        my_row = lax.axis_index("row")

        def give(act):
            for row, ids in enumerate(given_where):

                @pl.when(my_row == row)
                def _():
                    each = len(ids) // 2
                    for n, i in enumerate(ids):
                        target = solved_ref.at[n // each, pl.ds((n % each) * height, height)]
                        copy = pltpu.make_async_copy(given_refs[i], target, refs[4].at[n])
                        copy.start() if act else copy.wait()

        @pl.when(step == 0)
        def _():
            fetch(where, chunk_refs, whole, sems, height, my_row)
            hi, lo = split(whole[...])
            x_hi[...] = hi
            x_lo[...] = lo
            if last:
                give(True)

        j = js[0] + step // steps
        old = rhs_refs[0][0]
        for h, ref in enumerate(rhs_refs[1:]):
            old = jnp.where(j >= heads[0].shape[0], ref[0], old)
        live = j * len(where) + my_row > k
        done = j < 0
        for (panel, begin, end, piece, piece_end, row, _), (at, stop) in zip(parts, spans):
            active = live & (j >= begin) & (j < end)
            done |= active

            @pl.when(active)
            def _():
                if isinstance(panel, tuple):
                    even = lax.rem(col_ref[0], 2) == 0
                    pieces = []
                    for mine, other in zip(panel_refs[at:stop:2], panel_refs[at + 1:stop:2]):
                        a, b = mine[0, 0], other[0, 0]
                        pieces += [jnp.where(even, a, b), jnp.where(even, b, a)]
                else:
                    pieces = [panel_refs[at][p, 0] for p in range(piece_end - piece)]
                left = jnp.concatenate(pieces, axis=1)
                span = slice(row, row + left.shape[1])
                out_ref[0] = old - dot3(left, x_hi[span], x_lo[span])

        @pl.when(jnp.logical_not(done))
        def _():
            out_ref[0] = old

        if last:

            @pl.when(step == (js[1] - js[0]) * steps - 1)
            def _():
                give(False)

    block = pl.BlockSpec((1, tile, cols), lambda s, col: (js[0] + s // steps, s % steps, 0))
    kind = heads[0].dtype
    shape = (blocks, rows, cols)
    out_shape = [jax.ShapeDtypeStruct(shape, kind) if last else pltpu.HBM(shape, kind)]
    out_specs = [block]
    rhs_specs = [block]
    if len(heads) == 2:
        edge = heads[0].shape[0] * steps

        def before(s, col):
            at = jnp.minimum(s, edge - 1)
            return (at // steps, at % steps, 0)

        def beyond(s, col):
            at = jnp.maximum(s - edge, 0)
            return (at // steps, at % steps, 0)

        rhs_specs = [pl.BlockSpec((1, tile, cols), f) for f in (before, beyond)]
    if fresh:
        out_shape = [jax.ShapeDtypeStruct((js[1] - js[0], rows, cols), kind)]
        out_specs = [pl.BlockSpec((1, tile, cols), lambda s, col: (s // steps, s % steps, 0))]
    scratch = [
        pltpu.VMEM((depth, cols), jnp.float32),
        pltpu.VMEM((depth, cols), jnp.bfloat16),
        pltpu.VMEM((depth, cols), jnp.bfloat16),
        pltpu.SemaphoreType.DMA((len(where[0]),)),
    ]
    if last:
        out_shape.append(
            jax.ShapeDtypeStruct((2, height * len(given_where[0]) // 2, cols), kind)
        )
        out_specs.append(full(out_shape[-1].shape))
        scratch.append(pltpu.SemaphoreType.DMA((len(given_where[0]),)))
    outs = pl.pallas_call(
        kernel,
        grid_spec=pltpu.PrefetchScalarGridSpec(
            num_scalar_prefetch=1,
            grid=((js[1] - js[0]) * steps,),
            in_specs=rhs_specs + panel_specs + [ANY] * (len(arrays) + len(given) + len(after)),
            out_specs=out_specs,
            scratch_shapes=scratch,
        ),
        out_shape=out_shape,
        input_output_aliases={} if first or last or fresh else {1: 0},
        compiler_params=params(),
        cost_estimate=cost(),
    )(
        lax.axis_index("col").astype(jnp.int32).reshape(1),
        *[in_hbm(h) for h in heads],
        *[in_hbm(panel) for panel in panels],
        *[in_hbm(a) for a in arrays + given],
        *after,
    )
    return outs if last else outs[0]


def body(right_side, panel_t, inverse_blocks):
    n_row = lax.axis_size("row")
    n_col = lax.axis_size("col")
    blocks, _, cols = right_side.shape
    share = inverse_blocks.shape[1]
    half = share // 2
    n = inverse_blocks.shape[2] // share
    others = [q for q in range(n_row) if q != 1]

    def send(value, pairs):
        return lax.ppermute(value, "row", pairs)

    def swap(value):
        return lax.ppermute(value, "col", [(d, d ^ 1) for d in range(n_col)])

    def onward(value, t):
        rows = [0] if t < n else []
        rows += [r for r in range(1, n_row - 1) if 0 <= t - LAG * r < 2 * n]
        return send(value, [(r, r + 1) for r in rows])

    halves = [(half, (q + 1) * share) for q in others]

    def cut(k):
        def plan(refs, outs):
            my_row = lax.axis_index("row")
            at = pl.multiple_of(lax.rem(lax.axis_index("col"), 2) * half, half)
            return [
                (my_row == q, refs[0].at[k, pl.ds(at, half), pl.ds(0, (q + 1) * share)], out)
                for q, out in zip(others, outs)
            ]

        return plan

    def start(refs, outs):
        return cut(0)(refs, outs) + [
            (
                lax.axis_index("row") == 0,
                refs[1].at[0, pl.ds(t * share, share)],
                outs[len(others) + t],
            )
            for t in range(LAG)
        ]

    def to_solver(parts):
        return [send(part, [(q, 1)]) for q, part in zip(others, parts)]

    def whole(k, parts):
        inverse = [[part, swap(part)] for part in parts]
        inverse.insert(1, [inverse_blocks])
        return inverse

    slots = 2 * n + LAG * (n_row - 2)
    *parts, sent0, sent1 = copies(
        [inverse_blocks, right_side], halves + [(share, cols)] * LAG, start, []
    )
    sent = [sent0, sent1]
    received = [onward(sent[0], 0), onward(sent[1], 1)]
    arrived = to_solver(parts)
    inverse = [whole(0, arrived), None]

    slabs = jnp.transpose(panel_t, (0, 2, 1, 3))
    gathered = []
    for k in range(2):
        turned = turn(slabs, [(k, j) for j in range(blocks)], [sent0])
        gathered.append(lax.all_gather(turned, "col"))

    remaining = right_side
    lowered = None
    solved_here = [[], []]
    back = [[], []]
    after = arrived

    def chunks_of(k, first, end):
        rows_of = [back[k], solved_here[k]] + [
            received[k * n + LAG * (r - 1):][:n] for r in range(2, n_row)
        ]
        return [c[first:end] for c in rows_of]

    def to_first(k, first, end):
        both = send(jnp.concatenate(solved_here[k][first:end], axis=0), [(1, 0)])
        back[k] += [both[i * share:(i + 1) * share] for i in range(end - first)]

    late = LAG * (n_row - 2)
    for t in range(LAG, slots + LAG):
        value = received[t - LAG]
        k, q = divmod(t - LAG, n)
        if t < slots:
            if k < 2:
                rhs = received[: q + 1] if k == 0 else [lowered]
                top = right_side if t < n else None
                sent.append(slot(inverse[k][q], k, rhs, value, top, t, after))
                solved_here[k].append(sent[t])
            else:
                sent.append(value)
            received.append(onward(sent[t], t))
            after = []
        here = [sent[t]] if t < slots else []
        if t == LAG:
            arrived = to_solver(copies([inverse_blocks], halves, cut(1), here))
            inverse[1] = whole(1, arrived)
        if t == 2 * LAG:
            after = arrived
        if t == n + LAG - 1:
            lowered = update(
                right_side,
                -1,
                [(gathered[0], 0, 1, 0, n_col, 0, 0)],
                [solved_here[0]],
                here,
                (0, 1),
                fresh=True,
            )
            after = [lowered]
        if t == n + LAG:
            to_first(0, 0, n)
        if t in (n + LAG + 1, n + LAG + 3):
            to_first(1, t - n - LAG - 1, t - n - LAG + 1)
        ready = t - LAG - late
        if ready == n - 1:
            remaining = update(
                remaining,
                0,
                [(gathered[0], 0, 2, 0, n_col, 0, 0)],
                chunks_of(0, 0, n),
                here,
                (0, 2),
                fresh=True,
            )
            after = [remaining]
        if ready == n:
            third = update(
                right_side,
                0,
                [(gathered[0], 2, 3, 0, n_col, 0, 2)],
                chunks_of(0, 0, n),
                here,
                (2, 3),
                fresh=True,
            )
            after = [third]
    remaining, solved = update(
        [remaining, third],
        1,
        [(gathered[1], 0, blocks, 0, n_col, 0, 0)],
        chunks_of(1, 0, n),
        [],
        (0, blocks),
        solved=[[chunks_of(k, r, r + 1)[r] for r in range(n_row)] for k in range(2)],
    )
    return (solved, remaining)


def choose(right_side, panel_t, inverse_blocks):
    plane = lax.axis_size("col") == 8 and panel_t.shape[1] == 128
    if plane and inverse_blocks.shape[1] == 256 and lax.axis_size("row") == 4:
        return body(right_side, panel_t, inverse_blocks)
    return plain_body(right_side, panel_t, inverse_blocks)


def solution(mesh):
    return jax.shard_map(
        choose,
        mesh=mesh,
        in_specs=(P(None, "row", "col"), P(None, "col", None, "row"), P(None, "row", None)),
        out_specs=(P(None, "row", "col"), P(None, "row", "col")),
        check_vma=False,
    )
```

```python
import functools
import math

import jax
import jax.numpy as jnp
from jax import lax
from jax.experimental import pallas as pl
from jax.experimental.pallas import tpu as pltpu
from jax.sharding import PartitionSpec as P

def from_root(value, axis, source):
    kept = jnp.where(lax.axis_index(axis) == source, value, 0).astype(value.dtype)
    return lax.psum(kept, axis)


def plain_body(right_side, panel_t, inverse_blocks):
    grid_rows = lax.axis_size("row")
    my_row = lax.axis_index("row")
    blocks_here = right_side.shape[0]
    global_block = jnp.arange(blocks_here, dtype=jnp.int32) * grid_rows + my_row
    results = []
    for k in range(2):
        owner = k % grid_rows
        top = from_root(right_side[k // grid_rows], "row", owner)
        share = jnp.dot(
            inverse_blocks[k],
            top,
            precision=lax.Precision.HIGHEST,
            preferred_element_type=jnp.float32,
        )
        results.append(share)
        solved_k = lax.all_gather(share, "row", axis=0, tiled=True)
        update = jnp.einsum(
            "cji,cr->jir",
            lax.all_gather(panel_t[k], "col", axis=0, tiled=True),
            solved_k,
            precision=lax.Precision.HIGHEST,
            preferred_element_type=jnp.float32,
        )
        keep_mask = (global_block > k)[:, None, None]
        right_side = right_side - jnp.where(keep_mask, update, jnp.float32(0.0))
    return (jnp.stack(results), right_side)


VMEM_LIMIT = 20 * 2**20
LAG = 2


def split(x):
    hi = x.astype(jnp.bfloat16)
    return hi, (x - hi.astype(jnp.float32)).astype(jnp.bfloat16)


def dot3(a, b_hi, b_lo):
    a_hi, a_lo = split(a)
    dot = functools.partial(jnp.dot, preferred_element_type=jnp.float32)
    return dot(a_hi, b_hi) + (dot(a_hi, b_lo) + dot(a_lo, b_hi))


def in_vmem(x):
    return pltpu.with_memory_space_constraint(x, pltpu.VMEM)


ANY = pl.BlockSpec(memory_space=pl.ANY)
WHOLE = pl.BlockSpec(memory_space=pltpu.VMEM)


def distinct(sources):
    arrays = []
    where = []
    for chunks in sources:
        ids = []
        for chunk in chunks:
            for i, a in enumerate(arrays):
                if a is chunk:
                    break
            else:
                i = len(arrays)
                arrays.append(chunk)
            ids.append(i)
        where.append(ids)
    return arrays, where


def params(limit=VMEM_LIMIT):
    return pltpu.CompilerParams(vmem_limit_bytes=limit)


def cost():
    return pl.CostEstimate(flops=1024, bytes_accessed=1024, transcendentals=0)


def in_hbm(x):
    return pltpu.with_memory_space_constraint(x, pltpu.HBM)


def PIN(x):
    return x


def full(shape):
    return pl.BlockSpec(shape, lambda *_: (0,) * len(shape))


def copies(sources, shapes, plan, after):
    count = len(sources)

    def kernel(*refs):
        outs, sems = refs[-1 - len(shapes):-1], refs[-1]
        moves = plan(refs[:count], outs)
        for act in (True, False):
            for n, (condition, source, target) in enumerate(moves):

                def go():
                    copy = pltpu.make_async_copy(source, target, sems.at[n])
                    copy.start() if act else copy.wait()

                if condition is None:
                    go()
                else:
                    pl.when(condition)(go)

    return pl.pallas_call(
        kernel,
        grid=(1,),
        in_specs=[ANY] * (count + len(after)),
        out_specs=[full(shape) for shape in shapes],
        out_shape=[jax.ShapeDtypeStruct(shape, jnp.float32) for shape in shapes],
        scratch_shapes=[pltpu.SemaphoreType.DMA((16,))],
        compiler_params=params(),
        cost_estimate=cost(),
    )(*[in_hbm(x) for x in sources], *after)


def slot(inverse, k, rhs, received, top, part, after):
    cols = received.shape[1]
    packed = not isinstance(inverse, list)
    scratch = []
    if packed:
        chunk = depth = cols // 2
        specs = [ANY]
        scratch = [pltpu.VMEM((chunk, depth), jnp.float32)]
        inverse = [inverse]
    elif len(inverse) == 1:
        _, chunk, _ = inverse[0].shape
        depth = (part - LAG - k * (inverse[0].shape[2] // chunk) + 1) * chunk
        specs = [pl.BlockSpec((1, chunk, depth), lambda s: (k, 0, 0))]
        inverse = [in_hbm(inverse[0])]
    else:
        half, depth = inverse[0].shape
        chunk = 2 * half
        specs = [full((half, depth))] * 2
    tops = [] if top is None else [in_hbm(top[0])]

    def kernel(*refs):
        inverse_refs, refs = refs[: len(inverse)], refs[len(inverse):]
        received_ref, refs = refs[0], refs[1:]
        rhs_refs, refs = refs[: len(rhs)], refs[len(rhs):]
        out_ref, whole, sems = refs[-3 - len(scratch):][:3]
        my_row = lax.axis_index("row")

        def move(moves):
            copies = [
                pltpu.make_async_copy(source, target, sems.at[n])
                for n, (source, target) in enumerate(moves)
            ]
            for copy in copies:
                copy.start()
            for copy in copies:
                copy.wait()

        if tops:

            @pl.when(my_row == 0)
            def _():
                move(top[1](refs[0], out_ref))

        @pl.when(my_row == 1)
        def _():
            moves = []
            for n, ref in enumerate(rhs_refs):
                if ref.shape[0] == 1:
                    moves.append((ref.at[0, pl.ds(0, depth)], whole))
                else:
                    moves.append((ref.at[pl.ds(0, chunk)], whole.at[pl.ds(n * chunk, chunk)]))
            if packed and k == 0:
                moves += [
                    (
                        inverse_refs[0].at[pl.ds(chunk, chunk // 2), pl.ds(p * chunk, chunk)],
                        refs[-1].at[pl.ds(p * (chunk // 2), chunk // 2)],
                    )
                    for p in range(2)
                ]
            elif packed:
                moves.append((inverse_refs[0].at[:, pl.ds(0, chunk)], refs[-1]))
            move(moves)
            high, low = split(whole[...])
            if packed:
                out_ref[...] = dot3(refs[-1][...], high, low)
            elif len(inverse) == 1:
                out_ref[...] = dot3(inverse_refs[0][0], high, low)
            else:
                core = lax.rem(lax.axis_index("col"), 2)
                for p, ref in enumerate(inverse_refs):
                    at = pl.multiple_of((core if p == 0 else 1 - core) * half, half)
                    out_ref[pl.ds(at, half)] = dot3(ref[...], high, low)

        @pl.when(my_row > 1)
        def _():
            move([(received_ref.at[pl.ds(0, chunk)], out_ref)])

    return pl.pallas_call(
        kernel,
        grid=(1,),
        in_specs=specs + [ANY] * (1 + len(rhs) + len(tops) + len(after)),
        out_specs=full((chunk, cols)),
        out_shape=jax.ShapeDtypeStruct((chunk, cols), jnp.float32),
        scratch_shapes=[
            pltpu.VMEM((depth, cols), jnp.float32),
            pltpu.SemaphoreType.DMA((len(rhs) + 2,)),
        ]
        + scratch,
        compiler_params=params(),
        cost_estimate=cost(),
    )(*inverse, received, *rhs, *tops, *after)


def fetch(where, refs, whole, sems, height, my_row):
    for row, ids in enumerate(where):

        @pl.when((my_row == row) | (len(where) == 1))
        def _():
            copies = [
                pltpu.make_async_copy(refs[i], whole.at[pl.ds(n * height, height)], sems.at[n])
                for n, i in enumerate(ids)
            ]
            for copy in copies:
                copy.start()
            for copy in copies:
                copy.wait()


def update(rhs, k, parts, sources, after, js, first=False, fresh=False, solved=None):
    heads = rhs if isinstance(rhs, list) else [rhs]
    _, rows, cols = heads[0].shape
    blocks = max(h.shape[0] for h in heads)
    tile = 512
    steps = rows // tile
    arrays, where = distinct(sources)
    height = arrays[0].shape[0]
    depth = height * len(where[0])
    given, given_where = distinct([a + b for a, b in zip(*solved)]) if solved else ([], [])
    last = len(given) > 0
    panels = []
    panel_specs = []
    spans = []
    for panel, begin, end, piece, piece_end, _, slab in parts:

        def place(s, begin=begin, end=end, slab=slab):
            at = jnp.clip(s - (begin - js[0]) * steps, 0, (end - begin) * steps - 1)
            return slab + at // steps, at % steps

        at = len(panels)
        count = piece_end - piece

        def index(s, col, which=piece // count, place=place):
            return (which, *place(s), 0)

        panels.append(panel)
        panel_specs.append(pl.BlockSpec((count, 1, tile, panel.shape[3]), index))
        spans.append((at, len(panels)))

    def kernel(col_ref, *refs):
        rhs_refs, refs = refs[: len(heads)], refs[len(heads):]
        panel_refs, refs = refs[: len(panels)], refs[len(panels):]
        chunk_refs, refs = refs[: len(arrays)], refs[len(arrays):]
        given_refs, refs = refs[: len(given)], refs[len(given):]
        refs = refs[len(after):]
        out_ref, refs = refs[0], refs[1:]
        if last:
            solved_ref, refs = refs[0], refs[1:]
        whole, x_hi, x_lo, sems = refs[:4]
        step = pl.program_id(0)
        my_row = lax.axis_index("row")

        def give(act):
            for row, ids in enumerate(given_where):

                @pl.when(my_row == row)
                def _():
                    each = len(ids) // 2
                    for n, i in enumerate(ids):
                        target = solved_ref.at[n // each, pl.ds((n % each) * height, height)]
                        copy = pltpu.make_async_copy(given_refs[i], target, refs[4].at[n])
                        copy.start() if act else copy.wait()

        @pl.when(step == 0)
        def _():
            fetch(where, chunk_refs, whole, sems, height, my_row)
            hi, lo = split(whole[...])
            x_hi[...] = hi
            x_lo[...] = lo
            if last:
                give(True)

        j = js[0] + step // steps
        old = rhs_refs[0][0]
        for h, ref in enumerate(rhs_refs[1:]):
            old = jnp.where(j >= heads[0].shape[0], ref[0], old)
        live = j * len(where) + my_row > k
        out_ref[0] = old
        for (panel, begin, end, piece, piece_end, row, _), (at, stop) in zip(parts, spans):

            @pl.when(live & (j >= begin) & (j < end))
            def _():
                left = jnp.concatenate(
                    [panel_refs[at][p, 0] for p in range(piece_end - piece)], axis=1
                )
                span = slice(row, row + left.shape[1])
                out_ref[0] = out_ref[0] - dot3(left, x_hi[span], x_lo[span])

        if last:

            @pl.when(step == (js[1] - js[0]) * steps - 1)
            def _():
                give(False)

    block = pl.BlockSpec((1, tile, cols), lambda s, col: (js[0] + s // steps, s % steps, 0))
    kind = heads[0].dtype
    shape = (blocks, rows, cols)
    out_shape = [jax.ShapeDtypeStruct(shape, kind) if last else pltpu.HBM(shape, kind)]
    out_specs = [block]
    rhs_specs = [block]
    if len(heads) == 2:
        edge = heads[0].shape[0] * steps

        def before(s, col):
            at = jnp.minimum(s, edge - 1)
            return (at // steps, at % steps, 0)

        def beyond(s, col):
            at = jnp.maximum(s, edge)
            return (at // steps, at % steps, 0)

        rhs_specs = [pl.BlockSpec((1, tile, cols), f) for f in (before, beyond)]
    if fresh:
        out_shape = [jax.ShapeDtypeStruct((js[1] - js[0], rows, cols), kind)]
        if js[1] - js[0] == blocks:
            out_shape = [pltpu.HBM((blocks, rows, cols), kind)]
        out_specs = [pl.BlockSpec((1, tile, cols), lambda s, col: (s // steps, s % steps, 0))]
    scratch = [
        pltpu.VMEM((depth, cols), jnp.float32),
        pltpu.VMEM((depth, cols), jnp.bfloat16),
        pltpu.VMEM((depth, cols), jnp.bfloat16),
        pltpu.SemaphoreType.DMA((len(where[0]),)),
    ]
    if last:
        out_shape.append(
            jax.ShapeDtypeStruct((2, height * len(given_where[0]) // 2, cols), kind)
        )
        out_specs.append(full(out_shape[-1].shape))
        scratch.append(pltpu.SemaphoreType.DMA((len(given_where[0]),)))
    outs = pl.pallas_call(
        kernel,
        grid_spec=pltpu.PrefetchScalarGridSpec(
            num_scalar_prefetch=1,
            grid=((js[1] - js[0]) * steps,),
            in_specs=rhs_specs + panel_specs + [ANY] * (len(arrays) + len(given) + len(after)),
            out_specs=out_specs,
            scratch_shapes=scratch,
        ),
        out_shape=out_shape,
        input_output_aliases={} if first or last or fresh else {1: 0},
        compiler_params=params(2 * VMEM_LIMIT if last else VMEM_LIMIT),
        cost_estimate=cost(),
    )(
        lax.axis_index("col").astype(jnp.int32).reshape(1),
        *[in_hbm(h) for h in heads],
        *[in_hbm(panel) for panel in panels],
        *[in_hbm(a) for a in arrays + given],
        *after,
    )
    return outs if last else outs[0]


def body(right_side, panel_t, inverse_blocks):
    n_row = lax.axis_size("row")
    n_col = lax.axis_size("col")
    blocks, _, cols = right_side.shape
    share = inverse_blocks.shape[1]
    half = share // 2
    n = inverse_blocks.shape[2] // share
    others = list(range(2, n_row))

    def send(value, pairs):
        return lax.ppermute(value, "row", pairs)

    def swap(value, mask=1):
        return lax.ppermute(value, "col", [(d, d ^ mask) for d in range(n_col)])

    def onward(value, t):
        rows = [0] if t <= n else []
        rows += [r for r in range(1, n_row - 1) if 0 <= t - LAG * r < 2 * n]
        return send(value, [(r, r + 1) for r in rows])

    halves = [(half, (q + 1) * share) for q in others]

    def cut(k, wanted=others):
        def plan(refs, outs):
            my_row = lax.axis_index("row")
            at = pl.multiple_of(lax.rem(lax.axis_index("col"), 2) * half, half)
            return [
                (my_row == q, refs[0].at[k, pl.ds(at, half), pl.ds(0, (q + 1) * share)], out)
                for q, out in zip(wanted, outs)
            ]

        return plan

    def rows_of_top(t):
        return lambda ref, out: [(ref.at[0, pl.ds(t * share, share)], out)]

    def start(refs, outs):
        first, second, *parts = outs
        moves = [
            (refs[1].at[0, pl.ds(0, share)], first.at[pl.ds(0, share)]),
            (refs[1].at[0, pl.ds(share, share)], second),
        ] + [
            (
                refs[0].at[0, pl.ds(p * half, half), pl.ds(0, share)],
                first.at[pl.ds(share, half), pl.ds(p * share, share)],
            )
            for p in range(2)
        ]
        moves = [(lax.axis_index("row") == 0, *move) for move in moves]
        return moves + cut(0)(refs, parts)

    def to_solver(parts):
        return [send(part, [(q, 1)]) for q, part in zip(others, parts)]

    slots = 2 * n + LAG * (n_row - 2)

    turned = jnp.transpose(panel_t, (0, 2, 3, 1)).reshape(2 * blocks, -1, panel_t.shape[1])
    gathered = [lax.all_gather(turned[i:i + blocks], "col") for i in (0, blocks)]

    *sent, part2, part3 = copies(
        [inverse_blocks, right_side], [(share + half, cols), (share, cols)] + halves, start, []
    )
    received = [onward(sent[t], t) for t in range(LAG)]
    arrived = to_solver([part2, part3])
    inverse = [
        [received[0], [inverse_blocks]] + [[part, swap(part)] for part in arrived],
        [None, [inverse_blocks]],
    ]

    lowered = None
    solved_here = [[], []]
    back = []
    after = arrived

    def chunks_of(k, first, end):
        rows_of = [back[k * n:][:n], solved_here[k]] + [
            received[k * n + LAG * (r - 1):][:n] for r in range(2, n_row)
        ]
        return [c[first:end] for c in rows_of]

    for t in range(LAG, slots):
        value = received[t - LAG]
        k, q = divmod(t - LAG, n)
        if k < 2:
            rhs = received[: q + 1] if k == 0 else [lowered]
            top = None
            if t < n:
                top = right_side, rows_of_top(t)
            elif t == n:
                top = inverse_blocks, lambda ref, out: [
                    (ref.at[1, :, pl.ds(0, share)], out.at[:, pl.ds(0, share)])
                ]
            sent.append(slot(inverse[k][q], k, rhs, value, top, t, after))
            solved_here[k].append(sent[t])
            back.append(send(sent[t], [(1, 0)]))
        else:
            sent.append(value)
        received.append(onward(sent[t], t))
        after = back[t - 2 * LAG + 1:t - 2 * LAG + 2] if t >= 2 * LAG - 1 else []
        here = [sent[t]]
        if t in (2, 3):
            part, = copies([inverse_blocks], [halves[t - 2]], cut(1, [t]), here)
            arrived = send(part, [(t, 1)])
            inverse[1].append([arrived, swap(arrived)])
            after = after + [arrived]
        if t == n:
            inverse[1][0] = received[n]
        if t == n + LAG - 1:
            lowered = update(
                right_side,
                -1,
                [(gathered[0], 0, 1, 0, n_col, 0, 0)],
                [solved_here[0]],
                here,
                (0, 1),
                fresh=True,
            )
            after = after + [lowered]
        if t == slots - 1:
            remaining = update(
                right_side,
                0,
                [(gathered[0], 0, blocks, 0, n_col, 0, 0)],
                chunks_of(0, 0, n),
                here,
                (0, blocks),
                fresh=True,
            )
    remaining, solved = update(
        remaining,
        1,
        [(gathered[1], 0, blocks, 0, n_col, 0, 0)],
        chunks_of(1, 0, n),
        [],
        (0, blocks),
        solved=[[chunks_of(k, r, r + 1)[r] for r in range(n_row)] for k in range(2)],
    )
    return (solved, remaining)


def choose(right_side, panel_t, inverse_blocks):
    plane = lax.axis_size("col") == 8 and panel_t.shape[1] == 128
    if plane and inverse_blocks.shape[1] == 256 and lax.axis_size("row") == 4:
        return body(right_side, panel_t, inverse_blocks)
    return plain_body(right_side, panel_t, inverse_blocks)


def solution(mesh):
    return jax.shard_map(
        choose,
        mesh=mesh,
        in_specs=(P(None, "row", "col"), P(None, "col", None, "row"), P(None, "row", None)),
        out_specs=(P(None, "row", "col"), P(None, "row", "col")),
        check_vma=False,
    )
```

```python
import functools
import math

import jax
import jax.numpy as jnp
from jax import lax
from jax.experimental import pallas as pl
from jax.experimental.pallas import tpu as pltpu
from jax.sharding import PartitionSpec as P

def from_root(value, axis, source):
    kept = jnp.where(lax.axis_index(axis) == source, value, 0).astype(value.dtype)
    return lax.psum(kept, axis)


def plain_body(right_side, panel_t, inverse_blocks):
    grid_rows = lax.axis_size("row")
    my_row = lax.axis_index("row")
    blocks_here = right_side.shape[0]
    global_block = jnp.arange(blocks_here, dtype=jnp.int32) * grid_rows + my_row
    results = []
    for k in range(2):
        owner = k % grid_rows
        top = from_root(right_side[k // grid_rows], "row", owner)
        share = jnp.dot(
            inverse_blocks[k],
            top,
            precision=lax.Precision.HIGHEST,
            preferred_element_type=jnp.float32,
        )
        results.append(share)
        solved_k = lax.all_gather(share, "row", axis=0, tiled=True)
        update = jnp.einsum(
            "cji,cr->jir",
            lax.all_gather(panel_t[k], "col", axis=0, tiled=True),
            solved_k,
            precision=lax.Precision.HIGHEST,
            preferred_element_type=jnp.float32,
        )
        keep_mask = (global_block > k)[:, None, None]
        right_side = right_side - jnp.where(keep_mask, update, jnp.float32(0.0))
    return (jnp.stack(results), right_side)


VMEM_LIMIT = 20 * 2**20
LAG = 2


def split(x):
    hi = x.astype(jnp.bfloat16)
    return hi, (x - hi.astype(jnp.float32)).astype(jnp.bfloat16)


def dot3(a, b_hi, b_lo):
    a_hi, a_lo = split(a)
    dot = functools.partial(jnp.dot, preferred_element_type=jnp.float32)
    return dot(a_hi, b_hi) + (dot(a_hi, b_lo) + dot(a_lo, b_hi))


def in_vmem(x):
    return pltpu.with_memory_space_constraint(x, pltpu.VMEM)


ANY = pl.BlockSpec(memory_space=pl.ANY)
WHOLE = pl.BlockSpec(memory_space=pltpu.VMEM)


def distinct(sources):
    arrays = []
    where = []
    for chunks in sources:
        ids = []
        for chunk in chunks:
            for i, a in enumerate(arrays):
                if a is chunk:
                    break
            else:
                i = len(arrays)
                arrays.append(chunk)
            ids.append(i)
        where.append(ids)
    return arrays, where


def params(limit=VMEM_LIMIT):
    return pltpu.CompilerParams(vmem_limit_bytes=limit)


def cost():
    return pl.CostEstimate(flops=1024, bytes_accessed=1024, transcendentals=0)


def in_hbm(x):
    return pltpu.with_memory_space_constraint(x, pltpu.HBM)


def PIN(x):
    return x


def full(shape):
    return pl.BlockSpec(shape, lambda *_: (0,) * len(shape))


def copies(sources, shapes, plan, after):
    count = len(sources)

    def kernel(*refs):
        outs, sems = refs[-1 - len(shapes):-1], refs[-1]
        moves = plan(refs[:count], outs)
        for act in (True, False):
            for n, (condition, source, target) in enumerate(moves):

                def go():
                    copy = pltpu.make_async_copy(source, target, sems.at[n])
                    copy.start() if act else copy.wait()

                if condition is None:
                    go()
                else:
                    pl.when(condition)(go)

    return pl.pallas_call(
        kernel,
        grid=(1,),
        in_specs=[ANY] * (count + len(after)),
        out_specs=[full(shape) for shape in shapes],
        out_shape=[jax.ShapeDtypeStruct(shape, jnp.float32) for shape in shapes],
        scratch_shapes=[pltpu.SemaphoreType.DMA((16,))],
        compiler_params=params(),
        cost_estimate=cost(),
    )(*[in_hbm(x) for x in sources], *after)


def slot(inverse, k, rhs, received, top, part, after):
    cols = received.shape[1]
    packed = not isinstance(inverse, list)
    scratch = []
    if packed:
        chunk = depth = cols // 2
        specs = [ANY]
        scratch = [pltpu.VMEM((chunk, depth), jnp.float32)]
        inverse = [inverse]
    elif len(inverse) == 1:
        _, chunk, _ = inverse[0].shape
        depth = (part - LAG - k * (inverse[0].shape[2] // chunk) + 1) * chunk
        specs = [pl.BlockSpec((1, chunk, depth), lambda s: (k, 0, 0))]
        inverse = [in_hbm(inverse[0])]
    else:
        half, depth = inverse[0].shape
        chunk = 2 * half
        specs = [full((half, depth))] * 2
    tops = [] if top is None else [in_hbm(top[0])]

    def kernel(*refs):
        inverse_refs, refs = refs[: len(inverse)], refs[len(inverse):]
        received_ref, refs = refs[0], refs[1:]
        rhs_refs, refs = refs[: len(rhs)], refs[len(rhs):]
        out_ref, whole, sems = refs[-3 - len(scratch):][:3]
        my_row = lax.axis_index("row")

        def move(moves):
            copies = [
                pltpu.make_async_copy(source, target, sems.at[n])
                for n, (source, target) in enumerate(moves)
            ]
            for copy in copies:
                copy.start()
            for copy in copies:
                copy.wait()

        if tops:

            @pl.when(my_row == 0)
            def _():
                move(top[1](refs[0], out_ref))

        @pl.when(my_row == 1)
        def _():
            moves = []
            for n, ref in enumerate(rhs_refs):
                if ref.shape[0] == 1:
                    moves.append((ref.at[0, pl.ds(0, depth)], whole))
                else:
                    moves.append((ref.at[pl.ds(0, chunk)], whole.at[pl.ds(n * chunk, chunk)]))
            if packed and k == 0:
                moves += [
                    (
                        inverse_refs[0].at[pl.ds(chunk, chunk // 2), pl.ds(p * chunk, chunk)],
                        refs[-1].at[pl.ds(p * (chunk // 2), chunk // 2)],
                    )
                    for p in range(2)
                ]
            elif packed:
                moves.append((inverse_refs[0].at[:, pl.ds(0, chunk)], refs[-1]))
            move(moves)
            high, low = split(whole[...])
            if packed:
                out_ref[...] = dot3(refs[-1][...], high, low)
            elif len(inverse) == 1:
                out_ref[...] = dot3(inverse_refs[0][0], high, low)
            else:
                core = lax.rem(lax.axis_index("col"), 2)
                for p, ref in enumerate(inverse_refs):
                    at = pl.multiple_of((core if p == 0 else 1 - core) * half, half)
                    out_ref[pl.ds(at, half)] = dot3(ref[...], high, low)

        @pl.when(my_row > 1)
        def _():
            move([(received_ref.at[pl.ds(0, chunk)], out_ref)])

    return pl.pallas_call(
        kernel,
        grid=(1,),
        in_specs=specs + [ANY] * (1 + len(rhs) + len(tops) + len(after)),
        out_specs=full((chunk, cols)),
        out_shape=jax.ShapeDtypeStruct((chunk, cols), jnp.float32),
        scratch_shapes=[
            pltpu.VMEM((depth, cols), jnp.float32),
            pltpu.SemaphoreType.DMA((len(rhs) + 2,)),
        ]
        + scratch,
        compiler_params=params(),
        cost_estimate=cost(),
    )(*inverse, received, *rhs, *tops, *after)


def fetch(where, refs, whole, sems, height, my_row):
    for row, ids in enumerate(where):

        @pl.when((my_row == row) | (len(where) == 1))
        def _():
            copies = [
                pltpu.make_async_copy(refs[i], whole.at[pl.ds(n * height, height)], sems.at[n])
                for n, i in enumerate(ids)
            ]
            for copy in copies:
                copy.start()
            for copy in copies:
                copy.wait()


def update(rhs, k, parts, sources, after, js, first=False, fresh=False, solved=None):
    heads = rhs if isinstance(rhs, list) else [rhs]
    _, rows, cols = heads[0].shape
    blocks = max(h.shape[0] for h in heads)
    tile = 512
    steps = rows // tile
    arrays, where = distinct(sources)
    height = arrays[0].shape[0]
    depth = height * len(where[0])
    given, given_where = distinct([a + b for a, b in zip(*solved)]) if solved else ([], [])
    last = len(given) > 0
    panels = []
    panel_specs = []
    spans = []
    for panel, begin, end, piece, piece_end, _, slab in parts:

        def place(s, begin=begin, end=end, slab=slab):
            at = jnp.clip(s - (begin - js[0]) * steps, 0, (end - begin) * steps - 1)
            return slab + at // steps, at % steps

        at = len(panels)
        count = piece_end - piece

        def index(s, col, which=piece // count, place=place):
            return (which, *place(s), 0)

        panels.append(panel)
        panel_specs.append(pl.BlockSpec((count, 1, tile, panel.shape[3]), index))
        spans.append((at, len(panels)))

    def kernel(col_ref, *refs):
        rhs_refs, refs = refs[: len(heads)], refs[len(heads):]
        panel_refs, refs = refs[: len(panels)], refs[len(panels):]
        chunk_refs, refs = refs[: len(arrays)], refs[len(arrays):]
        given_refs, refs = refs[: len(given)], refs[len(given):]
        refs = refs[len(after):]
        out_ref, refs = refs[0], refs[1:]
        if last:
            solved_ref, refs = refs[0], refs[1:]
        whole, x_hi, x_lo, sems = refs[:4]
        step = pl.program_id(0)
        my_row = lax.axis_index("row")

        def give(act):
            for row, ids in enumerate(given_where):

                @pl.when(my_row == row)
                def _():
                    each = len(ids) // 2
                    for n, i in enumerate(ids):
                        target = solved_ref.at[n // each, pl.ds((n % each) * height, height)]
                        copy = pltpu.make_async_copy(given_refs[i], target, refs[4].at[n])
                        copy.start() if act else copy.wait()

        @pl.when(step == 0)
        def _():
            fetch(where, chunk_refs, whole, sems, height, my_row)
            hi, lo = split(whole[...])
            x_hi[...] = hi
            x_lo[...] = lo
            if last:
                give(True)

        j = js[0] + step // steps
        old = rhs_refs[0][0]
        for h, ref in enumerate(rhs_refs[1:]):
            old = jnp.where(j >= heads[0].shape[0], ref[0], old)
        live = j * len(where) + my_row > k
        out_ref[0] = old
        for (panel, begin, end, piece, piece_end, row, _), (at, stop) in zip(parts, spans):

            @pl.when(live & (j >= begin) & (j < end))
            def _():
                left = jnp.concatenate(
                    [panel_refs[at][p, 0] for p in range(piece_end - piece)], axis=1
                )
                span = slice(row, row + left.shape[1])
                out_ref[0] = out_ref[0] - dot3(left, x_hi[span], x_lo[span])

        if last:

            @pl.when(step == (js[1] - js[0]) * steps - 1)
            def _():
                give(False)

    block = pl.BlockSpec((1, tile, cols), lambda s, col: (js[0] + s // steps, s % steps, 0))
    kind = heads[0].dtype
    shape = (blocks, rows, cols)
    out_shape = [jax.ShapeDtypeStruct(shape, kind) if last else pltpu.HBM(shape, kind)]
    out_specs = [block]
    rhs_specs = [block]
    if len(heads) == 2:
        edge = heads[0].shape[0] * steps

        def before(s, col):
            at = jnp.minimum(s, edge - 1)
            return (at // steps, at % steps, 0)

        def beyond(s, col):
            at = jnp.maximum(s, edge)
            return (at // steps, at % steps, 0)

        rhs_specs = [pl.BlockSpec((1, tile, cols), f) for f in (before, beyond)]
    if fresh:
        out_shape = [jax.ShapeDtypeStruct((js[1] - js[0], rows, cols), kind)]
        if js[1] - js[0] > 1:
            out_shape = [pltpu.HBM((js[1] - js[0], rows, cols), kind)]
        out_specs = [pl.BlockSpec((1, tile, cols), lambda s, col: (s // steps, s % steps, 0))]
    scratch = [
        pltpu.VMEM((depth, cols), jnp.float32),
        pltpu.VMEM((depth, cols), jnp.bfloat16),
        pltpu.VMEM((depth, cols), jnp.bfloat16),
        pltpu.SemaphoreType.DMA((len(where[0]),)),
    ]
    if last:
        out_shape.append(
            jax.ShapeDtypeStruct((2, height * len(given_where[0]) // 2, cols), kind)
        )
        out_specs.append(full(out_shape[-1].shape))
        scratch.append(pltpu.SemaphoreType.DMA((len(given_where[0]),)))
    outs = pl.pallas_call(
        kernel,
        grid_spec=pltpu.PrefetchScalarGridSpec(
            num_scalar_prefetch=1,
            grid=((js[1] - js[0]) * steps,),
            in_specs=rhs_specs + panel_specs + [ANY] * (len(arrays) + len(given) + len(after)),
            out_specs=out_specs,
            scratch_shapes=scratch,
        ),
        out_shape=out_shape,
        input_output_aliases={} if first or last or fresh else {1: 0},
        compiler_params=params(2 * VMEM_LIMIT if last else VMEM_LIMIT),
        cost_estimate=cost(),
    )(
        lax.axis_index("col").astype(jnp.int32).reshape(1),
        *[in_hbm(h) for h in heads],
        *[in_hbm(panel) for panel in panels],
        *[in_hbm(a) for a in arrays + given],
        *after,
    )
    return outs if last else outs[0]


def body(right_side, panel_t, inverse_blocks):
    n_row = lax.axis_size("row")
    n_col = lax.axis_size("col")
    blocks, _, cols = right_side.shape
    share = inverse_blocks.shape[1]
    half = share // 2
    n = inverse_blocks.shape[2] // share
    others = list(range(2, n_row))

    def send(value, pairs):
        return lax.ppermute(value, "row", pairs)

    def swap(value, mask=1):
        return lax.ppermute(value, "col", [(d, d ^ mask) for d in range(n_col)])

    def onward(value, t):
        rows = [0] if t <= n else []
        rows += [r for r in range(1, n_row - 1) if 0 <= t - LAG * r < 2 * n]
        return send(value, [(r, r + 1) for r in rows])

    halves = [(half, (q + 1) * share) for q in others]

    def cut(k, wanted=others):
        def plan(refs, outs):
            my_row = lax.axis_index("row")
            at = pl.multiple_of(lax.rem(lax.axis_index("col"), 2) * half, half)
            return [
                (my_row == q, refs[0].at[k, pl.ds(at, half), pl.ds(0, (q + 1) * share)], out)
                for q, out in zip(wanted, outs)
            ]

        return plan

    def rows_of_top(t):
        return lambda ref, out: [(ref.at[0, pl.ds(t * share, share)], out)]

    def start(refs, outs):
        first, second, *parts = outs
        moves = [
            (refs[1].at[0, pl.ds(0, share)], first.at[pl.ds(0, share)]),
            (refs[1].at[0, pl.ds(share, share)], second),
        ] + [
            (
                refs[0].at[0, pl.ds(p * half, half), pl.ds(0, share)],
                first.at[pl.ds(share, half), pl.ds(p * share, share)],
            )
            for p in range(2)
        ]
        moves = [(lax.axis_index("row") == 0, *move) for move in moves]
        return moves + cut(0)(refs, parts)

    def to_solver(parts):
        return [send(part, [(q, 1)]) for q, part in zip(others, parts)]

    slots = 2 * n + LAG * (n_row - 2)

    turned = jnp.transpose(panel_t, (0, 2, 3, 1)).reshape(2 * blocks, -1, panel_t.shape[1])
    gathered = [lax.all_gather(turned[:2], "col"), lax.all_gather(turned[2:], "col")]

    *sent, part2, part3 = copies(
        [inverse_blocks, right_side], [(share + half, cols), (share, cols)] + halves, start, []
    )
    received = [onward(sent[t], t) for t in range(LAG)]
    arrived = to_solver([part2, part3])
    inverse = [
        [received[0], [inverse_blocks]] + [[part, swap(part)] for part in arrived],
        [None, [inverse_blocks]],
    ]

    lowered = None
    solved_here = [[], []]
    back = []
    after = arrived

    def chunks_of(k, first, end):
        rows_of = [back[k * n:][:n], solved_here[k]] + [
            received[k * n + LAG * (r - 1):][:n] for r in range(2, n_row)
        ]
        return [c[first:end] for c in rows_of]

    for t in range(LAG, slots):
        value = received[t - LAG]
        k, q = divmod(t - LAG, n)
        if k < 2:
            rhs = received[: q + 1] if k == 0 else [lowered]
            top = None
            if t < n:
                top = right_side, rows_of_top(t)
            elif t == n:
                top = inverse_blocks, lambda ref, out: [
                    (ref.at[1, :, pl.ds(0, share)], out.at[:, pl.ds(0, share)])
                ]
            sent.append(slot(inverse[k][q], k, rhs, value, top, t, after))
            solved_here[k].append(sent[t])
            back.append(send(sent[t], [(1, 0)]))
        else:
            sent.append(value)
        received.append(onward(sent[t], t))
        after = back[t - 2 * LAG + 1:t - 2 * LAG + 2] if t >= 2 * LAG - 1 else []
        here = [sent[t]]
        if t in (2, 3):
            part, = copies([inverse_blocks], [halves[t - 2]], cut(1, [t]), here)
            arrived = send(part, [(t, 1)])
            inverse[1].append([arrived, swap(arrived)])
        if t in (3, 4):
            after = after + inverse[1][t - 1][:1]
        if t == n:
            inverse[1][0] = received[n]
        if t == n + LAG - 1:
            lowered = update(
                right_side,
                -1,
                [(gathered[0], 0, 1, 0, n_col, 0, 0)],
                [solved_here[0]],
                here,
                (0, 1),
                fresh=True,
            )
            after = after + [lowered]
        if t == slots - 1:
            remaining = update(
                right_side,
                0,
                [(gathered[0], 0, 2, 0, n_col, 0, 0)],
                chunks_of(0, 0, n),
                here,
                (0, 2),
                fresh=True,
            )
    both = [x + y for x, y in zip(chunks_of(0, 0, n), chunks_of(1, 0, n))]
    remaining, solved = update(
        [remaining, right_side],
        1,
        [
            (gathered[1], 2, 3, 0, n_col, 0, 0),
            (gathered[1], 0, blocks, 0, n_col, n * share, 1),
        ],
        both,
        [],
        (0, blocks),
        solved=[[chunks_of(k, r, r + 1)[r] for r in range(n_row)] for k in range(2)],
    )
    return (solved, remaining)


def choose(right_side, panel_t, inverse_blocks):
    plane = lax.axis_size("col") == 8 and panel_t.shape[1] == 128
    if plane and inverse_blocks.shape[1] == 256 and lax.axis_size("row") == 4:
        return body(right_side, panel_t, inverse_blocks)
    return plain_body(right_side, panel_t, inverse_blocks)


def solution(mesh):
    return jax.shard_map(
        choose,
        mesh=mesh,
        in_specs=(P(None, "row", "col"), P(None, "col", None, "row"), P(None, "row", None)),
        out_specs=(P(None, "row", "col"), P(None, "row", "col")),
        check_vma=False,
    )
```

```python
import functools
import math

import jax
import jax.numpy as jnp
from jax import lax
from jax.experimental import pallas as pl
from jax.experimental.pallas import tpu as pltpu
from jax.sharding import PartitionSpec as P

def from_root(value, axis, source):
    kept = jnp.where(lax.axis_index(axis) == source, value, 0).astype(value.dtype)
    return lax.psum(kept, axis)


def plain_body(right_side, panel_t, inverse_blocks):
    grid_rows = lax.axis_size("row")
    my_row = lax.axis_index("row")
    blocks_here = right_side.shape[0]
    global_block = jnp.arange(blocks_here, dtype=jnp.int32) * grid_rows + my_row
    results = []
    for k in range(2):
        owner = k % grid_rows
        top = from_root(right_side[k // grid_rows], "row", owner)
        share = jnp.dot(
            inverse_blocks[k],
            top,
            precision=lax.Precision.HIGHEST,
            preferred_element_type=jnp.float32,
        )
        results.append(share)
        solved_k = lax.all_gather(share, "row", axis=0, tiled=True)
        update = jnp.einsum(
            "cji,cr->jir",
            lax.all_gather(panel_t[k], "col", axis=0, tiled=True),
            solved_k,
            precision=lax.Precision.HIGHEST,
            preferred_element_type=jnp.float32,
        )
        keep_mask = (global_block > k)[:, None, None]
        right_side = right_side - jnp.where(keep_mask, update, jnp.float32(0.0))
    return (jnp.stack(results), right_side)


VMEM_LIMIT = 20 * 2**20
LAG = 2


def split(x):
    hi = x.astype(jnp.bfloat16)
    return hi, (x - hi.astype(jnp.float32)).astype(jnp.bfloat16)


def dot3(a, b_hi, b_lo):
    a_hi, a_lo = split(a)
    dot = functools.partial(jnp.dot, preferred_element_type=jnp.float32)
    return dot(a_hi, b_hi) + (dot(a_hi, b_lo) + dot(a_lo, b_hi))


def in_vmem(x):
    return pltpu.with_memory_space_constraint(x, pltpu.VMEM)


ANY = pl.BlockSpec(memory_space=pl.ANY)
WHOLE = pl.BlockSpec(memory_space=pltpu.VMEM)


def distinct(sources):
    arrays = []
    where = []
    for chunks in sources:
        ids = []
        for chunk in chunks:
            for i, a in enumerate(arrays):
                if a is chunk:
                    break
            else:
                i = len(arrays)
                arrays.append(chunk)
            ids.append(i)
        where.append(ids)
    return arrays, where


def params(limit=VMEM_LIMIT):
    return pltpu.CompilerParams(vmem_limit_bytes=limit)


def cost():
    return pl.CostEstimate(flops=1024, bytes_accessed=1024, transcendentals=0)


def in_hbm(x):
    return pltpu.with_memory_space_constraint(x, pltpu.HBM)


def PIN(x):
    return x


def full(shape):
    return pl.BlockSpec(shape, lambda *_: (0,) * len(shape))


def copies(sources, shapes, plan, after):
    count = len(sources)

    def kernel(*refs):
        outs, sems = refs[-1 - len(shapes):-1], refs[-1]
        moves = plan(refs[:count], outs)
        for act in (True, False):
            for n, (condition, source, target) in enumerate(moves):

                def go():
                    copy = pltpu.make_async_copy(source, target, sems.at[n])
                    copy.start() if act else copy.wait()

                if condition is None:
                    go()
                else:
                    pl.when(condition)(go)

    return pl.pallas_call(
        kernel,
        grid=(1,),
        in_specs=[ANY] * (count + len(after)),
        out_specs=[full(shape) for shape in shapes],
        out_shape=[jax.ShapeDtypeStruct(shape, jnp.float32) for shape in shapes],
        scratch_shapes=[pltpu.SemaphoreType.DMA((16,))],
        compiler_params=params(),
        cost_estimate=cost(),
    )(*[in_hbm(x) for x in sources], *after)


def slot(inverse, k, rhs, received, top, part, after):
    cols = received.shape[1]
    packed = not isinstance(inverse, list)
    scratch = []
    if packed:
        chunk = depth = cols // 2
        specs = [ANY]
        scratch = [pltpu.VMEM((chunk, depth), jnp.float32)]
        inverse = [inverse]
    elif len(inverse) == 1:
        _, chunk, _ = inverse[0].shape
        depth = (part - LAG - k * (inverse[0].shape[2] // chunk) + 1) * chunk
        specs = [pl.BlockSpec((1, chunk, depth), lambda s: (k, 0, 0))]
        inverse = [in_hbm(inverse[0])]
    else:
        half, depth = inverse[0].shape
        chunk = 2 * half
        specs = [full((half, depth))] * 2
    tops = [] if top is None else [in_hbm(top[0])]

    def kernel(*refs):
        inverse_refs, refs = refs[: len(inverse)], refs[len(inverse):]
        received_ref, refs = refs[0], refs[1:]
        rhs_refs, refs = refs[: len(rhs)], refs[len(rhs):]
        out_ref, whole, sems = refs[-3 - len(scratch):][:3]
        my_row = lax.axis_index("row")

        def move(moves):
            copies = [
                pltpu.make_async_copy(source, target, sems.at[n])
                for n, (source, target) in enumerate(moves)
            ]
            for copy in copies:
                copy.start()
            for copy in copies:
                copy.wait()

        if tops:

            @pl.when(my_row == 0)
            def _():
                move(top[1](refs[0], out_ref))

        @pl.when(my_row == 1)
        def _():
            moves = []
            for n, ref in enumerate(rhs_refs):
                if ref.shape[0] == 1:
                    moves.append((ref.at[0, pl.ds(0, depth)], whole))
                else:
                    moves.append((ref.at[pl.ds(0, chunk)], whole.at[pl.ds(n * chunk, chunk)]))
            if packed and k == 0:
                moves += [
                    (
                        inverse_refs[0].at[pl.ds(chunk, chunk // 2), pl.ds(p * chunk, chunk)],
                        refs[-1].at[pl.ds(p * (chunk // 2), chunk // 2)],
                    )
                    for p in range(2)
                ]
            elif packed:
                moves.append((inverse_refs[0].at[:, pl.ds(0, chunk)], refs[-1]))
            move(moves)
            high, low = split(whole[...])
            if packed:
                out_ref[...] = dot3(refs[-1][...], high, low)
            elif len(inverse) == 1:
                out_ref[...] = dot3(inverse_refs[0][0], high, low)
            else:
                core = lax.rem(lax.axis_index("col"), 2)
                for p, ref in enumerate(inverse_refs):
                    at = pl.multiple_of((core if p == 0 else 1 - core) * half, half)
                    out_ref[pl.ds(at, half)] = dot3(ref[...], high, low)

        @pl.when(my_row > 1)
        def _():
            move([(received_ref.at[pl.ds(0, chunk)], out_ref)])

    return pl.pallas_call(
        kernel,
        grid=(1,),
        in_specs=specs + [ANY] * (1 + len(rhs) + len(tops) + len(after)),
        out_specs=full((chunk, cols)),
        out_shape=jax.ShapeDtypeStruct((chunk, cols), jnp.float32),
        scratch_shapes=[
            pltpu.VMEM((depth, cols), jnp.float32),
            pltpu.SemaphoreType.DMA((len(rhs) + 2,)),
        ]
        + scratch,
        compiler_params=params(),
        cost_estimate=cost(),
    )(*inverse, received, *rhs, *tops, *after)


def fetch(where, refs, whole, sems, height, my_row, first, end, start, wait):
    for row, ids in enumerate(where):

        @pl.when((my_row == row) | (len(where) == 1))
        def _():
            copies = [
                pltpu.make_async_copy(refs[ids[n]], whole.at[pl.ds(n * height, height)], sems.at[n])
                for n in range(first, end)
            ]
            for copy in copies if start else []:
                copy.start()
            for copy in copies if wait else []:
                copy.wait()


def update(rhs, k, parts, sources, after, js, first=False, fresh=False, solved=None):
    heads = rhs if isinstance(rhs, list) else [rhs]
    _, rows, cols = heads[0].shape
    blocks = max(h.shape[0] for h in heads)
    tile = 512
    steps = rows // tile
    arrays, where = distinct(sources)
    height = arrays[0].shape[0]
    chunks = len(where[0])
    depth = height * chunks
    late = min(part[5] for part in parts[1:]) // height if len(parts) > 1 else 0
    given, given_where = distinct([a + b for a, b in zip(*solved)]) if solved else ([], [])
    last = len(given) > 0
    panels = []
    panel_specs = []
    spans = []
    for panel, begin, end, piece, piece_end, _, slab in parts:

        def place(s, begin=begin, end=end, slab=slab):
            at = jnp.clip(s - (begin - js[0]) * steps, 0, (end - begin) * steps - 1)
            return slab + at // steps, at % steps

        at = len(panels)
        count = piece_end - piece

        def index(s, col, which=piece // count, place=place):
            return (which, *place(s), 0)

        panels.append(panel)
        panel_specs.append(pl.BlockSpec((count, 1, tile, panel.shape[3]), index))
        spans.append((at, len(panels)))

    def kernel(col_ref, *refs):
        rhs_refs, refs = refs[: len(heads)], refs[len(heads):]
        panel_refs, refs = refs[: len(panels)], refs[len(panels):]
        chunk_refs, refs = refs[: len(arrays)], refs[len(arrays):]
        given_refs, refs = refs[: len(given)], refs[len(given):]
        refs = refs[len(after):]
        out_ref, refs = refs[0], refs[1:]
        if last:
            solved_ref, refs = refs[0], refs[1:]
        whole, x_hi, x_lo, sems = refs[:4]
        step = pl.program_id(0)
        my_row = lax.axis_index("row")

        def give(act):
            for row, ids in enumerate(given_where):

                @pl.when(my_row == row)
                def _():
                    each = len(ids) // 2
                    for n, i in enumerate(ids):
                        target = solved_ref.at[n // each, pl.ds((n % each) * height, height)]
                        copy = pltpu.make_async_copy(given_refs[i], target, refs[4].at[n])
                        copy.start() if act else copy.wait()

        @pl.when(step == 0)
        def _():
            fetch(where, chunk_refs, whole, sems, height, my_row, late, chunks, True, False)
            fetch(where, chunk_refs, whole, sems, height, my_row, 0, late, True, False)
            fetch(where, chunk_refs, whole, sems, height, my_row, late, chunks, False, True)
            hi, lo = split(whole[late * height:])
            x_hi[late * height:] = hi
            x_lo[late * height:] = lo
            if last:
                give(True)

        if late:

            @pl.when(step == (parts[0][1] - js[0]) * steps)
            def _():
                fetch(where, chunk_refs, whole, sems, height, my_row, 0, late, False, True)
                hi, lo = split(whole[:late * height])
                x_hi[:late * height] = hi
                x_lo[:late * height] = lo

        j = js[0] + step // steps
        old = rhs_refs[0][0]
        for h, ref in enumerate(rhs_refs[1:]):
            old = jnp.where(j >= heads[0].shape[0], ref[0], old)
        live = j * len(where) + my_row > k
        out_ref[0] = old
        for (panel, begin, end, piece, piece_end, row, _), (at, stop) in zip(parts, spans):

            @pl.when(live & (j >= begin) & (j < end))
            def _():
                left = jnp.concatenate(
                    [panel_refs[at][p, 0] for p in range(piece_end - piece)], axis=1
                )
                span = slice(row, row + left.shape[1])
                out_ref[0] = out_ref[0] - dot3(left, x_hi[span], x_lo[span])

        if last:

            @pl.when(step == (js[1] - js[0]) * steps - 1)
            def _():
                give(False)

    block = pl.BlockSpec((1, tile, cols), lambda s, col: (js[0] + s // steps, s % steps, 0))
    kind = heads[0].dtype
    shape = (blocks, rows, cols)
    out_shape = [jax.ShapeDtypeStruct(shape, kind) if last else pltpu.HBM(shape, kind)]
    out_specs = [block]
    rhs_specs = [block]
    if len(heads) == 2:
        edge = heads[0].shape[0] * steps

        def before(s, col):
            at = jnp.minimum(s, edge - 1)
            return (at // steps, at % steps, 0)

        def beyond(s, col):
            at = jnp.maximum(s, edge)
            return (at // steps, at % steps, 0)

        rhs_specs = [pl.BlockSpec((1, tile, cols), f) for f in (before, beyond)]
    if fresh:
        out_shape = [jax.ShapeDtypeStruct((js[1] - js[0], rows, cols), kind)]
        if js[1] - js[0] > 1:
            out_shape = [pltpu.HBM((js[1] - js[0], rows, cols), kind)]
        out_specs = [pl.BlockSpec((1, tile, cols), lambda s, col: (s // steps, s % steps, 0))]
    scratch = [
        pltpu.VMEM((depth, cols), jnp.float32),
        pltpu.VMEM((depth, cols), jnp.bfloat16),
        pltpu.VMEM((depth, cols), jnp.bfloat16),
        pltpu.SemaphoreType.DMA((len(where[0]),)),
    ]
    if last:
        out_shape.append(
            jax.ShapeDtypeStruct((2, height * len(given_where[0]) // 2, cols), kind)
        )
        out_specs.append(full(out_shape[-1].shape))
        scratch.append(pltpu.SemaphoreType.DMA((len(given_where[0]),)))
    outs = pl.pallas_call(
        kernel,
        grid_spec=pltpu.PrefetchScalarGridSpec(
            num_scalar_prefetch=1,
            grid=((js[1] - js[0]) * steps,),
            in_specs=rhs_specs + panel_specs + [ANY] * (len(arrays) + len(given) + len(after)),
            out_specs=out_specs,
            scratch_shapes=scratch,
        ),
        out_shape=out_shape,
        input_output_aliases={} if first or last or fresh else {1: 0},
        compiler_params=params(2 * VMEM_LIMIT if last else VMEM_LIMIT),
        cost_estimate=cost(),
    )(
        lax.axis_index("col").astype(jnp.int32).reshape(1),
        *[in_hbm(h) for h in heads],
        *[in_hbm(panel) for panel in panels],
        *[in_hbm(a) for a in arrays + given],
        *after,
    )
    return outs if last else outs[0]


def body(right_side, panel_t, inverse_blocks):
    n_row = lax.axis_size("row")
    n_col = lax.axis_size("col")
    blocks, _, cols = right_side.shape
    share = inverse_blocks.shape[1]
    half = share // 2
    n = inverse_blocks.shape[2] // share
    others = list(range(2, n_row))

    def send(value, pairs):
        return lax.ppermute(value, "row", pairs)

    def swap(value, mask=1):
        return lax.ppermute(value, "col", [(d, d ^ mask) for d in range(n_col)])

    def onward(value, t):
        rows = [0] if t <= n else []
        rows += [r for r in range(1, n_row - 1) if 0 <= t - LAG * r < 2 * n]
        return send(value, [(r, r + 1) for r in rows])

    halves = [(half, (q + 1) * share) for q in others]

    def cut(k, wanted=others):
        def plan(refs, outs):
            my_row = lax.axis_index("row")
            at = pl.multiple_of(lax.rem(lax.axis_index("col"), 2) * half, half)
            return [
                (my_row == q, refs[0].at[k, pl.ds(at, half), pl.ds(0, (q + 1) * share)], out)
                for q, out in zip(wanted, outs)
            ]

        return plan

    def rows_of_top(t):
        return lambda ref, out: [(ref.at[0, pl.ds(t * share, share)], out)]

    def start(refs, outs):
        first, second, *parts = outs
        moves = [
            (refs[1].at[0, pl.ds(0, share)], first.at[pl.ds(0, share)]),
            (refs[1].at[0, pl.ds(share, share)], second),
        ] + [
            (
                refs[0].at[0, pl.ds(p * half, half), pl.ds(0, share)],
                first.at[pl.ds(share, half), pl.ds(p * share, share)],
            )
            for p in range(2)
        ]
        moves = [(lax.axis_index("row") == 0, *move) for move in moves]
        return moves + cut(0)(refs, parts)

    def to_solver(parts):
        return [send(part, [(q, 1)]) for q, part in zip(others, parts)]

    slots = 2 * n + LAG * (n_row - 2)

    turned = jnp.transpose(panel_t, (0, 2, 3, 1)).reshape(2 * blocks, -1, panel_t.shape[1])
    gathered = [lax.all_gather(turned[:2], "col"), lax.all_gather(turned[2:], "col")]

    *sent, part2, part3 = copies(
        [inverse_blocks, right_side], [(share + half, cols), (share, cols)] + halves, start, []
    )
    received = [onward(sent[t], t) for t in range(LAG)]
    arrived = to_solver([part2, part3])
    inverse = [
        [received[0], [inverse_blocks]] + [[part, swap(part)] for part in arrived],
        [None, [inverse_blocks]],
    ]

    lowered = None
    solved_here = [[], []]
    back = []
    after = arrived

    def chunks_of(k, first, end):
        rows_of = [back[k * n:][:n], solved_here[k]] + [
            received[k * n + LAG * (r - 1):][:n] for r in range(2, n_row)
        ]
        return [c[first:end] for c in rows_of]

    for t in range(LAG, slots):
        value = received[t - LAG]
        k, q = divmod(t - LAG, n)
        if k < 2:
            rhs = received[: q + 1] if k == 0 else [lowered]
            top = None
            if t < n:
                top = right_side, rows_of_top(t)
            elif t == n:
                top = inverse_blocks, lambda ref, out: [
                    (ref.at[1, :, pl.ds(0, share)], out.at[:, pl.ds(0, share)])
                ]
            sent.append(slot(inverse[k][q], k, rhs, value, top, t, after))
            solved_here[k].append(sent[t])
            back.append(send(sent[t], [(1, 0)]))
        else:
            sent.append(value)
        received.append(onward(sent[t], t))
        after = back[t - 2 * LAG + 1:t - 2 * LAG + 2] if t >= 2 * LAG - 1 else []
        here = [sent[t]]
        if t in (2, 3):
            part, = copies([inverse_blocks], [halves[t - 2]], cut(1, [t]), here)
            arrived = send(part, [(t, 1)])
            inverse[1].append([arrived, swap(arrived)])
        if t in (3, 4):
            after = after + inverse[1][t - 1][:1]
        if t == n:
            inverse[1][0] = received[n]
        if t == n + LAG - 1:
            lowered = update(
                right_side,
                -1,
                [(gathered[0], 0, 1, 0, n_col, 0, 0)],
                [solved_here[0]],
                here,
                (0, 1),
                fresh=True,
            )
            after = after + [lowered]
        if t == slots - 1:
            remaining = update(
                right_side,
                0,
                [(gathered[0], 0, 2, 0, n_col, 0, 0)],
                chunks_of(0, 0, n),
                here,
                (0, 2),
                fresh=True,
            )
    both = [x + y for x, y in zip(chunks_of(0, 0, n), chunks_of(1, 0, n))]
    remaining, solved = update(
        [remaining, right_side],
        1,
        [
            (gathered[1], 2, 3, 0, n_col, 0, 0),
            (gathered[1], 0, blocks, 0, n_col, n * share, 1),
        ],
        both,
        [],
        (0, blocks),
        solved=[[chunks_of(k, r, r + 1)[r] for r in range(n_row)] for k in range(2)],
    )
    return (solved, remaining)


def choose(right_side, panel_t, inverse_blocks):
    plane = lax.axis_size("col") == 8 and panel_t.shape[1] == 128
    if plane and inverse_blocks.shape[1] == 256 and lax.axis_size("row") == 4:
        return body(right_side, panel_t, inverse_blocks)
    return plain_body(right_side, panel_t, inverse_blocks)


def solution(mesh):
    return jax.shard_map(
        choose,
        mesh=mesh,
        in_specs=(P(None, "row", "col"), P(None, "col", None, "row"), P(None, "row", None)),
        out_specs=(P(None, "row", "col"), P(None, "row", "col")),
        check_vma=False,
    )
```

```python
import functools
import math

import jax
import jax.numpy as jnp
from jax import lax
from jax.experimental import pallas as pl
from jax.experimental.pallas import tpu as pltpu
from jax.sharding import PartitionSpec as P

def from_root(value, axis, source):
    kept = jnp.where(lax.axis_index(axis) == source, value, 0).astype(value.dtype)
    return lax.psum(kept, axis)


def plain_body(right_side, panel_t, inverse_blocks):
    grid_rows = lax.axis_size("row")
    my_row = lax.axis_index("row")
    blocks_here = right_side.shape[0]
    global_block = jnp.arange(blocks_here, dtype=jnp.int32) * grid_rows + my_row
    results = []
    for k in range(2):
        owner = k % grid_rows
        top = from_root(right_side[k // grid_rows], "row", owner)
        share = jnp.dot(
            inverse_blocks[k],
            top,
            precision=lax.Precision.HIGHEST,
            preferred_element_type=jnp.float32,
        )
        results.append(share)
        solved_k = lax.all_gather(share, "row", axis=0, tiled=True)
        update = jnp.einsum(
            "cji,cr->jir",
            lax.all_gather(panel_t[k], "col", axis=0, tiled=True),
            solved_k,
            precision=lax.Precision.HIGHEST,
            preferred_element_type=jnp.float32,
        )
        keep_mask = (global_block > k)[:, None, None]
        right_side = right_side - jnp.where(keep_mask, update, jnp.float32(0.0))
    return (jnp.stack(results), right_side)


VMEM_LIMIT = 20 * 2**20
LAG = 2


def split(x):
    hi = x.astype(jnp.bfloat16)
    return hi, (x - hi.astype(jnp.float32)).astype(jnp.bfloat16)


def dot3(a, b_hi, b_lo):
    a_hi, a_lo = split(a)
    dot = functools.partial(jnp.dot, preferred_element_type=jnp.float32)
    return dot(a_hi, b_hi) + (dot(a_hi, b_lo) + dot(a_lo, b_hi))


def in_vmem(x):
    return pltpu.with_memory_space_constraint(x, pltpu.VMEM)


ANY = pl.BlockSpec(memory_space=pl.ANY)
WHOLE = pl.BlockSpec(memory_space=pltpu.VMEM)


def distinct(sources):
    arrays = []
    where = []
    for chunks in sources:
        ids = []
        for chunk in chunks:
            for i, a in enumerate(arrays):
                if a is chunk:
                    break
            else:
                i = len(arrays)
                arrays.append(chunk)
            ids.append(i)
        where.append(ids)
    return arrays, where


def params(limit=VMEM_LIMIT):
    return pltpu.CompilerParams(vmem_limit_bytes=limit)


def cost():
    return pl.CostEstimate(flops=1024, bytes_accessed=1024, transcendentals=0)


def in_hbm(x):
    return pltpu.with_memory_space_constraint(x, pltpu.HBM)


def PIN(x):
    return x


def full(shape):
    return pl.BlockSpec(shape, lambda *_: (0,) * len(shape))


def copies(sources, shapes, plan, after):
    count = len(sources)

    def kernel(*refs):
        outs, sems = refs[-1 - len(shapes):-1], refs[-1]
        moves = plan(refs[:count], outs)
        for act in (True, False):
            for n, (condition, source, target) in enumerate(moves):

                def go():
                    copy = pltpu.make_async_copy(source, target, sems.at[n])
                    copy.start() if act else copy.wait()

                if condition is None:
                    go()
                else:
                    pl.when(condition)(go)

    return pl.pallas_call(
        kernel,
        grid=(1,),
        in_specs=[ANY] * (count + len(after)),
        out_specs=[full(shape) for shape in shapes],
        out_shape=[jax.ShapeDtypeStruct(shape, jnp.float32) for shape in shapes],
        scratch_shapes=[pltpu.SemaphoreType.DMA((16,))],
        compiler_params=params(),
        cost_estimate=cost(),
    )(*[in_hbm(x) for x in sources], *after)


def slot(inverse, k, rhs, received, top, part, after):
    cols = received.shape[1]
    packed = not isinstance(inverse, list)
    scratch = []
    if packed:
        chunk = depth = cols // 2
        specs = [ANY]
        scratch = [pltpu.VMEM((chunk, depth), jnp.float32)]
        inverse = [inverse]
    elif len(inverse) == 1:
        _, chunk, _ = inverse[0].shape
        depth = (part - LAG - k * (inverse[0].shape[2] // chunk) + 1) * chunk
        specs = [pl.BlockSpec((1, chunk, depth), lambda s: (k, 0, 0))]
        inverse = [in_hbm(inverse[0])]
    else:
        half, depth = inverse[0].shape
        chunk = 2 * half
        specs = [full((half, depth))] * 2
    tops = [] if top is None else [in_hbm(top[0])]

    def kernel(*refs):
        inverse_refs, refs = refs[: len(inverse)], refs[len(inverse):]
        received_ref, refs = refs[0], refs[1:]
        rhs_refs, refs = refs[: len(rhs)], refs[len(rhs):]
        out_ref, whole, sems = refs[-3 - len(scratch):][:3]
        my_row = lax.axis_index("row")

        def move(moves):
            copies = [
                pltpu.make_async_copy(source, target, sems.at[n])
                for n, (source, target) in enumerate(moves)
            ]
            for copy in copies:
                copy.start()
            for copy in copies:
                copy.wait()

        if tops:

            @pl.when(my_row == 0)
            def _():
                move(top[1](refs[0], out_ref))

        @pl.when(my_row == 1)
        def _():
            moves = []
            for n, ref in enumerate(rhs_refs):
                if ref.shape[0] == 1:
                    moves.append((ref.at[0, pl.ds(0, depth)], whole))
                else:
                    moves.append((ref.at[pl.ds(0, chunk)], whole.at[pl.ds(n * chunk, chunk)]))
            if packed and k == 0:
                moves += [
                    (
                        inverse_refs[0].at[pl.ds(chunk, chunk // 2), pl.ds(p * chunk, chunk)],
                        refs[-1].at[pl.ds(p * (chunk // 2), chunk // 2)],
                    )
                    for p in range(2)
                ]
            elif packed:
                moves.append((inverse_refs[0].at[:, pl.ds(0, chunk)], refs[-1]))
            move(moves)
            high, low = split(whole[...])
            if packed:
                out_ref[...] = dot3(refs[-1][...], high, low)
            elif len(inverse) == 1:
                out_ref[...] = dot3(inverse_refs[0][0], high, low)
            else:
                core = lax.rem(lax.axis_index("col"), 2)
                for p, ref in enumerate(inverse_refs):
                    at = pl.multiple_of((core if p == 0 else 1 - core) * half, half)
                    out_ref[pl.ds(at, half)] = dot3(ref[...], high, low)

        @pl.when(my_row > 1)
        def _():
            move([(received_ref.at[pl.ds(0, chunk)], out_ref)])

    return pl.pallas_call(
        kernel,
        grid=(1,),
        in_specs=specs + [ANY] * (1 + len(rhs) + len(tops) + len(after)),
        out_specs=full((chunk, cols)),
        out_shape=jax.ShapeDtypeStruct((chunk, cols), jnp.float32),
        scratch_shapes=[
            pltpu.VMEM((depth, cols), jnp.float32),
            pltpu.SemaphoreType.DMA((len(rhs) + 2,)),
        ]
        + scratch,
        compiler_params=params(),
        cost_estimate=cost(),
    )(*inverse, received, *rhs, *tops, *after)


def fetch(where, refs, whole, sems, height, my_row, first, end, start, wait):
    for row, ids in enumerate(where):

        @pl.when((my_row == row) | (len(where) == 1))
        def _():
            copies = [
                pltpu.make_async_copy(refs[ids[n]], whole.at[pl.ds(n * height, height)], sems.at[n])
                for n in range(first, end)
            ]
            for copy in copies if start else []:
                copy.start()
            for copy in copies if wait else []:
                copy.wait()


def update(rhs, k, parts, sources, after, js, first=False, fresh=False, solved=None):
    heads = rhs if isinstance(rhs, list) else [rhs]
    _, rows, cols = heads[0].shape
    blocks = max(h.shape[0] for h in heads)
    tile = 512
    steps = rows // tile
    arrays, where = distinct(sources)
    height = arrays[0].shape[0]
    chunks = len(where[0])
    depth = height * chunks
    late = min(part[5] for part in parts[1:]) // height if len(parts) > 1 else 0
    given, given_where = distinct([a + b for a, b in zip(*solved)]) if solved else ([], [])
    last = len(given) > 0
    panels = []
    panel_specs = []
    spans = []
    for panel, begin, end, piece, piece_end, _, slab in parts:

        def place(s, begin=begin, end=end, slab=slab):
            at = jnp.clip(s - (begin - js[0]) * steps, 0, (end - begin) * steps - 1)
            return slab + at // steps, at % steps

        at = len(panels)
        count = piece_end - piece

        def index(s, col, which=piece // count, place=place):
            return (which, *place(s), 0)

        panels.append(panel)
        panel_specs.append(pl.BlockSpec((count, 1, tile, panel.shape[3]), index))
        spans.append((at, len(panels)))

    def kernel(col_ref, *refs):
        rhs_refs, refs = refs[: len(heads)], refs[len(heads):]
        panel_refs, refs = refs[: len(panels)], refs[len(panels):]
        chunk_refs, refs = refs[: len(arrays)], refs[len(arrays):]
        given_refs, refs = refs[: len(given)], refs[len(given):]
        refs = refs[len(after):]
        out_ref, refs = refs[0], refs[1:]
        if last:
            solved_ref, refs = refs[0], refs[1:]
        whole, x_hi, x_lo, sems = refs[:4]
        step = pl.program_id(0)
        my_row = lax.axis_index("row")

        def give(act):
            for row, ids in enumerate(given_where):

                @pl.when(my_row == row)
                def _():
                    each = len(ids) // 2
                    for n, i in enumerate(ids):
                        target = solved_ref.at[n // each, pl.ds((n % each) * height, height)]
                        copy = pltpu.make_async_copy(given_refs[i], target, refs[4].at[n])
                        copy.start() if act else copy.wait()

        @pl.when(step == 0)
        def _():
            fetch(where, chunk_refs, whole, sems, height, my_row, late, chunks, True, False)
            fetch(where, chunk_refs, whole, sems, height, my_row, 0, late, True, False)
            for n in range(late, chunks):
                fetch(where, chunk_refs, whole, sems, height, my_row, n, n + 1, False, True)
                rows_n = slice(n * height, (n + 1) * height)
                hi, lo = split(whole[rows_n])
                x_hi[rows_n] = hi
                x_lo[rows_n] = lo
            if last:
                give(True)

        if late:

            @pl.when(step == (parts[0][1] - js[0]) * steps)
            def _():
                fetch(where, chunk_refs, whole, sems, height, my_row, 0, late, False, True)
                hi, lo = split(whole[:late * height])
                x_hi[:late * height] = hi
                x_lo[:late * height] = lo

        j = js[0] + step // steps
        old = rhs_refs[0][0]
        for h, ref in enumerate(rhs_refs[1:]):
            old = jnp.where(j >= heads[0].shape[0], ref[0], old)
        live = j * len(where) + my_row > k
        out_ref[0] = old
        for (panel, begin, end, piece, piece_end, row, _), (at, stop) in zip(parts, spans):

            @pl.when(live & (j >= begin) & (j < end))
            def _():
                left = jnp.concatenate(
                    [panel_refs[at][p, 0] for p in range(piece_end - piece)], axis=1
                )
                span = slice(row, row + left.shape[1])
                out_ref[0] = out_ref[0] - dot3(left, x_hi[span], x_lo[span])

        if last:

            @pl.when(step == (js[1] - js[0]) * steps - 1)
            def _():
                give(False)

    block = pl.BlockSpec((1, tile, cols), lambda s, col: (js[0] + s // steps, s % steps, 0))
    kind = heads[0].dtype
    shape = (blocks, rows, cols)
    out_shape = [jax.ShapeDtypeStruct(shape, kind) if last else pltpu.HBM(shape, kind)]
    out_specs = [block]
    rhs_specs = [block]
    if len(heads) == 2:
        edge = heads[0].shape[0] * steps

        def before(s, col):
            at = jnp.minimum(s, edge - 1)
            return (at // steps, at % steps, 0)

        def beyond(s, col):
            at = jnp.maximum(s, edge)
            return (at // steps, at % steps, 0)

        rhs_specs = [pl.BlockSpec((1, tile, cols), f) for f in (before, beyond)]
    if fresh:
        out_shape = [jax.ShapeDtypeStruct((js[1] - js[0], rows, cols), kind)]
        if js[1] - js[0] > 1:
            out_shape = [pltpu.HBM((js[1] - js[0], rows, cols), kind)]
        out_specs = [pl.BlockSpec((1, tile, cols), lambda s, col: (s // steps, s % steps, 0))]
    scratch = [
        pltpu.VMEM((depth, cols), jnp.float32),
        pltpu.VMEM((depth, cols), jnp.bfloat16),
        pltpu.VMEM((depth, cols), jnp.bfloat16),
        pltpu.SemaphoreType.DMA((len(where[0]),)),
    ]
    if last:
        out_shape.append(
            jax.ShapeDtypeStruct((2, height * len(given_where[0]) // 2, cols), kind)
        )
        out_specs.append(full(out_shape[-1].shape))
        scratch.append(pltpu.SemaphoreType.DMA((len(given_where[0]),)))
    outs = pl.pallas_call(
        kernel,
        grid_spec=pltpu.PrefetchScalarGridSpec(
            num_scalar_prefetch=1,
            grid=((js[1] - js[0]) * steps,),
            in_specs=rhs_specs + panel_specs + [ANY] * (len(arrays) + len(given) + len(after)),
            out_specs=out_specs,
            scratch_shapes=scratch,
        ),
        out_shape=out_shape,
        input_output_aliases={} if first or last or fresh else {1: 0},
        compiler_params=params(2 * VMEM_LIMIT if last else VMEM_LIMIT),
        cost_estimate=cost(),
    )(
        lax.axis_index("col").astype(jnp.int32).reshape(1),
        *[in_hbm(h) for h in heads],
        *[in_hbm(panel) for panel in panels],
        *[in_hbm(a) for a in arrays + given],
        *after,
    )
    return outs if last else outs[0]


def body(right_side, panel_t, inverse_blocks):
    n_row = lax.axis_size("row")
    n_col = lax.axis_size("col")
    blocks, _, cols = right_side.shape
    share = inverse_blocks.shape[1]
    half = share // 2
    n = inverse_blocks.shape[2] // share
    others = list(range(2, n_row))

    def send(value, pairs):
        return lax.ppermute(value, "row", pairs)

    def swap(value, mask=1):
        return lax.ppermute(value, "col", [(d, d ^ mask) for d in range(n_col)])

    def onward(value, t):
        rows = [0] if t <= n else []
        rows += [r for r in range(1, n_row - 1) if 0 <= t - LAG * r < 2 * n]
        return send(value, [(r, r + 1) for r in rows])

    halves = [(half, (q + 1) * share) for q in others]

    def cut(k, wanted=others):
        def plan(refs, outs):
            my_row = lax.axis_index("row")
            at = pl.multiple_of(lax.rem(lax.axis_index("col"), 2) * half, half)
            return [
                (my_row == q, refs[0].at[k, pl.ds(at, half), pl.ds(0, (q + 1) * share)], out)
                for q, out in zip(wanted, outs)
            ]

        return plan

    def rows_of_top(t):
        return lambda ref, out: [(ref.at[0, pl.ds(t * share, share)], out)]

    def start(refs, outs):
        first, second, *parts = outs
        moves = [
            (refs[1].at[0, pl.ds(0, share)], first.at[pl.ds(0, share)]),
            (refs[1].at[0, pl.ds(share, share)], second),
        ] + [
            (
                refs[0].at[0, pl.ds(p * half, half), pl.ds(0, share)],
                first.at[pl.ds(share, half), pl.ds(p * share, share)],
            )
            for p in range(2)
        ]
        moves = [(lax.axis_index("row") == 0, *move) for move in moves]
        return moves + cut(0)(refs, parts)

    def to_solver(parts):
        return [send(part, [(q, 1)]) for q, part in zip(others, parts)]

    slots = 2 * n + LAG * (n_row - 2)

    turned = jnp.transpose(panel_t, (0, 2, 3, 1)).reshape(2 * blocks, -1, panel_t.shape[1])
    gathered = [lax.all_gather(turned[:2], "col"), lax.all_gather(turned[2:], "col")]

    *sent, part2, part3 = copies(
        [inverse_blocks, right_side], [(share + half, cols), (share, cols)] + halves, start, []
    )
    received = [onward(sent[t], t) for t in range(LAG)]
    arrived = to_solver([part2, part3])
    inverse = [
        [received[0], [inverse_blocks]] + [[part, swap(part)] for part in arrived],
        [None, [inverse_blocks]],
    ]

    lowered = None
    solved_here = [[], []]
    back = []
    after = arrived

    def chunks_of(k, first, end):
        rows_of = [back[k * n:][:n], solved_here[k]] + [
            received[k * n + LAG * (r - 1):][:n] for r in range(2, n_row)
        ]
        return [c[first:end] for c in rows_of]

    for t in range(LAG, slots):
        value = received[t - LAG]
        k, q = divmod(t - LAG, n)
        if k < 2:
            rhs = received[: q + 1] if k == 0 else [lowered]
            top = None
            if t < n:
                top = right_side, rows_of_top(t)
            elif t == n:
                top = inverse_blocks, lambda ref, out: [
                    (ref.at[1, :, pl.ds(0, share)], out.at[:, pl.ds(0, share)])
                ]
            sent.append(slot(inverse[k][q], k, rhs, value, top, t, after))
            solved_here[k].append(sent[t])
            back.append(send(sent[t], [(1, 0)]))
        else:
            sent.append(value)
        received.append(onward(sent[t], t))
        after = back[t - 2 * LAG + 1:t - 2 * LAG + 2] if t >= 2 * LAG - 1 else []
        here = [sent[t]]
        if t in (2, 3):
            part, = copies([inverse_blocks], [halves[t - 2]], cut(1, [t]), here)
            arrived = send(part, [(t, 1)])
            inverse[1].append([arrived, swap(arrived)])
        if t in (3, 4):
            after = after + inverse[1][t - 1][:1]
        if t == n:
            inverse[1][0] = received[n]
        if t == n + LAG - 1:
            lowered = update(
                right_side,
                -1,
                [(gathered[0], 0, 1, 0, n_col, 0, 0)],
                [solved_here[0]],
                here,
                (0, 1),
                fresh=True,
            )
            after = after + [lowered]
        if t == slots - 1:
            remaining = update(
                right_side,
                0,
                [(gathered[0], 0, 2, 0, n_col, 0, 0)],
                chunks_of(0, 0, n),
                here,
                (0, 2),
                fresh=True,
            )
    both = [x + y for x, y in zip(chunks_of(0, 0, n), chunks_of(1, 0, n))]
    remaining, solved = update(
        [remaining, right_side],
        1,
        [
            (gathered[1], 2, 3, 0, n_col, 0, 0),
            (gathered[1], 0, blocks, 0, n_col, n * share, 1),
        ],
        both,
        [],
        (0, blocks),
        solved=[[chunks_of(k, r, r + 1)[r] for r in range(n_row)] for k in range(2)],
    )
    return (solved, remaining)


def choose(right_side, panel_t, inverse_blocks):
    plane = lax.axis_size("col") == 8 and panel_t.shape[1] == 128
    if plane and inverse_blocks.shape[1] == 256 and lax.axis_size("row") == 4:
        return body(right_side, panel_t, inverse_blocks)
    return plain_body(right_side, panel_t, inverse_blocks)


def solution(mesh):
    return jax.shard_map(
        choose,
        mesh=mesh,
        in_specs=(P(None, "row", "col"), P(None, "col", None, "row"), P(None, "row", None)),
        out_specs=(P(None, "row", "col"), P(None, "row", "col")),
        check_vma=False,
    )
```
